128 devices in a mesh: grp: 8 (over y, core), tp: 16 (over z, x).
Axes of the slice: x: 4, y: 4, z: 4, core: 2. Of those that a mesh axis runs over, the one named last changes fastest.
Arguments:
- states: bfloat16 [16384, 1280], P(('grp', 'tp')), may hold values from -6 to 6
- patch_of: int32 [16384], P(('grp', 'tp')), may hold values from 0 to 47, as said below
- targets: int32 [16384], P(('grp', 'tp')), may hold values from 0 to 255
- cotangent: float32 [16384], P(('grp', 'tp')), may hold values from -6 to 6
- w_in: bfloat16 [1280, 4096], P(None, 'tp'), may hold values from -0.15625 to 0.15625
- w_gate: bfloat16 [4096, 7168], P('grp', 'tp'), may hold values from -0.09375 to 0.09375
- w_up: bfloat16 [4096, 7168], P('grp', 'tp'), may hold values from -0.09375 to 0.09375
- w_down: bfloat16 [7168, 4096], P('tp', 'grp'), may hold values from -0.0625 to 0.0625
- w_out: bfloat16 [4096, 1280], P('tp'), may hold values from -0.09375 to 0.09375
- head_gain: float32 [1280], replicated, may hold values from 0.25 to 1.75
- w_head: bfloat16 [1280, 256], replicated, may hold values from -0.5 to 0.5
Outputs:
- log_probs: float32 [16384], P(('grp', 'tp'))
- state_grads: float32 [16384, 1280], P(('grp', 'tp'))
The draws below stay inside these ranges and needn't reach their ends.
Inputs may be any that keep to these rules, and one draw needn't show every extreme that they name: `patch_of`: within each device's block of 128 bytes the patch number is 0 at the first byte, never falls and rises by at most one from byte to byte. A device holds at most 48 patches; each aligned block of 8 devices, in the order grp then tp, holds exactly 224 patches in all, and one device of each such block holds 48.
All inputs are finite; a program needn't handle non-finite values.
Results may differ from the reference program's by a relative error of at most 0.023.
Values may be sent and summed in bfloat16 or wider, within the bound.
A program may use at most 128 MiB of HBM per device.

```python
import math
import jax
import jax.numpy as jnp
import numpy as np
from jax import lax

E = 1280
D = 4096
FF = 7168
V = 256
BYTES_DEV = 128
CAP_DEV = 48
PATCH_AVG = 28
BYTES = 16384
N_GRP = 8
N_TP = 16


def shuffle_eight(subkey):
    return jax.random.permutation(subkey, 8)


def shuffle_cuts(subkey):
    return jax.random.permutation(subkey, BYTES_DEV - 1)


def draw_patch_of(key, part):
    key = jax.random.fold_in(key, 11)
    devices = BYTES // BYTES_DEV
    blocks = devices // 8
    scale_unit = BYTES_DEV // 32
    profile = jnp.array([12, 10, 8, 7, 6, 5, 4, 4], jnp.int32) * scale_unit
    key_order, key_cut = jax.random.split(key)
    shuffle = jax.vmap(shuffle_eight)(jax.random.split(key_order, blocks))
    counts = jnp.take(profile, shuffle.reshape(devices), axis=0)
    rank_table = jax.vmap(shuffle_cuts)(jax.random.split(key_cut, devices))
    starts = (rank_table < counts[:, None] - 1).astype(jnp.int32)
    patch_ids = jnp.concatenate([jnp.zeros((devices, 1), jnp.int32), jnp.cumsum(starts, axis=1)], axis=1)
    return patch_ids.reshape(BYTES).astype(jnp.int32)


def touch_ends(entries, stream_key, low, largest):
    spot = [jax.random.randint(jax.random.fold_in(stream_key, axis), (), 0, length) for axis, length in enumerate(entries.shape)]
    main_axis = entries.shape.index(max(entries.shape))
    beside = spot[:main_axis] + [(spot[main_axis] + 1) % entries.shape[main_axis]] + spot[main_axis + 1:]
    return entries.at[tuple(spot)].set(low).at[tuple(beside)].set(largest)


def steps_of(key, shape, cuts, least, high):
    def one(dim, blocks):
        steps = jax.random.uniform(jax.random.fold_in(jax.random.fold_in(key, 6), dim), (blocks,), jnp.float32, least / len(cuts), high / len(cuts))
        return jnp.repeat(jnp.exp(steps), shape[dim] // blocks).reshape((-1,) + (1,) * (len(shape) - dim - 1))

    gain = one(*cuts[0])
    for cut in cuts[1:]:
        gain = gain * one(*cut)
    return gain


def cumulative_ranks(count, skew):
    weights = [(1 << 20) // math.isqrt(standing ** skew) + 1 for standing in range(1, count + 1)]
    scale = 1 + sum(weights) // (1 << 30)
    return np.cumsum(np.array([max(1, weight // scale) for weight in weights]))


def ranked_ids(stream_key, shape, number_of, skew):
    grid = cumulative_ranks(number_of, skew)
    ticket = jax.random.randint(jax.random.fold_in(stream_key, 1), shape, 0, int(grid[number_of - 1]))
    standing = jnp.searchsorted(jnp.asarray(grid, jnp.int32), ticket, side="right")
    return jax.random.permutation(jax.random.fold_in(stream_key, 2), number_of)[standing].astype(jnp.int32)


def centred(rng, shape, scale, most, cuts=(), kind=jnp.bfloat16):
    level = steps_of(rng, shape, cuts, -0.22, 0.18) if cuts else 1.0
    result = jax.random.normal(rng, shape, jnp.float32) * scale * level
    return jnp.minimum(jnp.maximum(result, -most), most).astype(kind)


def setup_inputs(seed: int = 0) -> dict:
    key_list = jax.random.split(jax.random.key(seed), 12)
    states = centred(key_list[0], (BYTES, E), 1.0, 6.0, ((0, 128),))
    patch_of = draw_patch_of(jax.random.fold_in(key_list[11], 71), 0)
    targets = touch_ends(ranked_ids(key_list[2], (BYTES,), V, 2), jax.random.fold_in(key_list[2], 3), 0, V - 1).astype(jnp.int32)
    cotangent = centred(key_list[3], (BYTES,), 1.0, 6.0, ((0, 128),), jnp.float32)
    w_in = centred(key_list[4], (E, D), E ** -0.5, 0.15625, ((1, 16),))
    w_gate = centred(key_list[5], (D, FF), D ** -0.5, 0.09375, ((0, 8), (1, 16)))
    w_up = centred(key_list[6], (D, FF), D ** -0.5, 0.09375, ((0, 8), (1, 16)))
    w_down = centred(key_list[7], (FF, D), FF ** -0.5, 0.0625, ((0, 16), (1, 8)))
    w_out = centred(key_list[8], (D, E), D ** -0.5, 0.09375, ((0, 16),))
    head_gain = jnp.clip(1.0 + 0.15 * jax.random.normal(key_list[9], (E,), jnp.float32), 0.25, 1.75)
    w_head = centred(key_list[10], (E, V), (E // 9) ** -0.5, 0.5)
    return dict(states=states, patch_of=patch_of, targets=targets, cotangent=cotangent, w_in=w_in, w_gate=w_gate, w_up=w_up, w_down=w_down, w_out=w_out, head_gain=head_gain, w_head=w_head)


def shard_sum(term_fn, shards, out_shape):

    def add_shard(shard_index, total_acc):
        shard_term = lax.optimization_barrier(term_fn(shard_index).astype(jnp.bfloat16))
        return total_acc + shard_term.astype(jnp.float32)
    return lax.fori_loop(0, shards, add_shard, jnp.zeros(out_shape, jnp.float32))

def contract(left_op, right_op, left_dim, right_dim):
    return lax.dot_general(left_op, right_op, (((left_dim,), (right_dim,)), ((), ())), preferred_element_type=jnp.float32)

def reference(states, patch_of, targets, cotangent, w_in, w_gate, w_up, w_down, w_out, head_gain, w_head):
    devices = N_GRP * N_TP
    capacity = CAP_DEV
    live_total = devices * PATCH_AVG
    feat_width = D // N_TP
    hidden_width = FF // N_TP
    highest = lax.Precision.HIGHEST
    slot_ids = jnp.arange(capacity, dtype=jnp.int32)
    member = patch_of.reshape(devices, 1, BYTES_DEV) == slot_ids[None, :, None]
    member_f32 = member.astype(jnp.float32)
    patch_sizes = lax.optimization_barrier(jnp.sum(member_f32, axis=2))
    divisor = jnp.maximum(patch_sizes, 1.0)
    state_rows = states.reshape(devices, BYTES_DEV, E).astype(jnp.float32)
    pooled = (jnp.einsum('dcb,dbe->dce', member_f32, state_rows, precision=highest) / divisor[:, :, None]).astype(jnp.bfloat16)
    live_index = jnp.nonzero(patch_sizes.reshape(-1) > 0, size=live_total)[0].astype(jnp.int32)
    flat_pooled = jnp.take(pooled.reshape(devices * capacity, E), live_index, axis=0)
    input_act = jnp.dot(flat_pooled, w_in, preferred_element_type=jnp.float32).astype(jnp.bfloat16)
    gate_pre = jnp.dot(input_act, w_gate, preferred_element_type=jnp.float32)
    up_pre = jnp.dot(input_act, w_up, preferred_element_type=jnp.float32)
    sigmoid_gate = jax.nn.sigmoid(gate_pre)
    hidden = (gate_pre * sigmoid_gate * up_pre).astype(jnp.bfloat16)

    def down_term(shard_index):
        begin_at = (shard_index * hidden_width).astype(jnp.int32)
        part_hidden = lax.dynamic_slice_in_dim(hidden, begin_at, hidden_width, 1)
        part_weight = lax.dynamic_slice_in_dim(w_down, begin_at, hidden_width, 0)
        return jnp.dot(part_hidden, part_weight, preferred_element_type=jnp.float32)
    mixed = (input_act.astype(jnp.float32) + shard_sum(down_term, N_TP, (live_total, D))).astype(jnp.bfloat16)

    def out_term(shard_index):
        begin_at = (shard_index * feat_width).astype(jnp.int32)
        part_mixed = lax.dynamic_slice_in_dim(mixed, begin_at, feat_width, 1)
        part_weight = lax.dynamic_slice_in_dim(w_out, begin_at, feat_width, 0)
        return jnp.dot(part_mixed, part_weight, preferred_element_type=jnp.float32)
    patch_out = shard_sum(out_term, N_TP, (live_total, E)).astype(jnp.bfloat16)
    home_out = jnp.zeros((devices * capacity, E), jnp.bfloat16).at[live_index].set(patch_out).reshape(devices, capacity, E)
    gathered = jnp.einsum('dcb,dce->dbe', member_f32, home_out.astype(jnp.float32), precision=highest)
    decoder_in = state_rows + gathered
    inverse = lax.rsqrt(lax.optimization_barrier(jnp.mean(decoder_in * decoder_in, axis=2, keepdims=True)) + 1e-06)
    normal_part = decoder_in * inverse
    normed = (normal_part * head_gain).astype(jnp.bfloat16).reshape(devices * BYTES_DEV, E)
    logits = jnp.dot(normed, w_head, preferred_element_type=jnp.float32)
    log_total = jnp.log(lax.optimization_barrier(jnp.sum(jnp.exp(logits), axis=1)))
    is_target = jnp.arange(V, dtype=jnp.int32)[None, :] == targets[:, None]
    chosen = lax.optimization_barrier(jnp.sum(jnp.where(is_target, logits, 0.0), axis=1))
    log_probs = chosen - log_total
    softmax_probs = jnp.exp(logits - log_total[:, None])
    logit_grads = (cotangent[:, None] * (is_target.astype(jnp.float32) - softmax_probs)).astype(jnp.bfloat16)
    scaled = (contract(logit_grads, w_head, 1, 1) * head_gain).reshape(devices, BYTES_DEV, E)
    decoder_grads = inverse * (scaled - normal_part * lax.optimization_barrier(jnp.mean(scaled * normal_part, axis=2, keepdims=True)))
    patch_grads = jnp.einsum('dcb,dbe->dce', member_f32, decoder_grads, precision=highest).astype(jnp.bfloat16)
    flat_grads = jnp.take(patch_grads.reshape(devices * capacity, E), live_index, axis=0)
    mixed_grads = contract(flat_grads, w_out, 1, 1).astype(jnp.bfloat16)
    hidden_grads = contract(mixed_grads, w_down, 1, 1)
    gate_grads = (hidden_grads * up_pre * sigmoid_gate * (1.0 + gate_pre * (1.0 - sigmoid_gate))).astype(jnp.bfloat16)
    up_grads = (hidden_grads * gate_pre * sigmoid_gate).astype(jnp.bfloat16)

    def input_term(shard_index):
        begin_at = (shard_index * hidden_width).astype(jnp.int32)
        part_gate = lax.dynamic_slice_in_dim(gate_grads, begin_at, hidden_width, 1)
        part_up = lax.dynamic_slice_in_dim(up_grads, begin_at, hidden_width, 1)
        gate_cols = lax.dynamic_slice_in_dim(w_gate, begin_at, hidden_width, 1)
        up_cols = lax.dynamic_slice_in_dim(w_up, begin_at, hidden_width, 1)
        return contract(part_gate, gate_cols, 1, 1) + contract(part_up, up_cols, 1, 1)
    input_grads = (mixed_grads.astype(jnp.float32) + shard_sum(input_term, N_TP, (live_total, D))).astype(jnp.bfloat16)

    def pooled_term(shard_index):
        begin_at = (shard_index * feat_width).astype(jnp.int32)
        part_grads = lax.dynamic_slice_in_dim(input_grads, begin_at, feat_width, 1)
        part_weight = lax.dynamic_slice_in_dim(w_in, begin_at, feat_width, 1)
        return contract(part_grads, part_weight, 1, 1)
    pooled_grads = shard_sum(pooled_term, N_TP, (live_total, E)).astype(jnp.bfloat16)
    home_grads = jnp.zeros((devices * capacity, E), jnp.bfloat16).at[live_index].set(pooled_grads).reshape(devices, capacity, E)
    byte_divisor = jnp.einsum('dcb,dc->db', member_f32, divisor, precision=highest)
    spread = jnp.einsum('dcb,dce->dbe', member_f32, home_grads.astype(jnp.float32), precision=highest) / byte_divisor[:, :, None]
    state_grads = (decoder_grads + spread).reshape(BYTES, E)
    return (log_probs, state_grads)
```

```python
import jax
import jax.numpy as jnp
from jax import lax
from jax.experimental import pallas as pl
from jax.experimental.pallas import tpu as pltpu
from jax.sharding import PartitionSpec as P

BF = jnp.bfloat16
F32 = jnp.float32
MESH = pl.DeviceIdType.MESH
SIDE = 4
SLOTS = 48
N_SEMS = 160


def nn(a, b):
    return lax.dot_general(a, b, (((1,), (0,)), ((), ())), preferred_element_type=F32)


def nt(a, b):
    return lax.dot_general(a, b, (((1,), (1,)), ((), ())), preferred_element_type=F32)


def wrap(v):
    return lax.rem(v, SIDE)


def kernel(
    states, patch_row, patch_col, targets, cotangent, w_in, w_gate, w_up, w_down, w_out, gain, w_head,
    log_probs, state_grads,
    raw_g, raw_u, raw_d, slab_in, slab_out, pool, fold_g, fold_u, fold_d,
    part_g, part_u, part_d, edge_g, edge_u, edge_d, mid_g, mid_u, mid_d,
    act, gate_c, up_c, hid, pout, qout, g_gate, g_up, g_mix, grads,
    rs1, rs2, mid1,
    ssem, rsem,
):
    E = states.shape[1]
    EH = E // 2
    FB = w_gate.shape[1]
    DG = w_gate.shape[0]
    DT = w_in.shape[1]
    ER = EH // SIDE
    FR = FB // SIDE
    OR = DT // SIDE
    ROWS = SIDE * SLOTS

    g = lax.axis_index("grp")
    t = lax.axis_index("tp")
    y, c = g // 2, g % 2
    z, x = t // SIDE, t % SIDE

    def X(d):
        return (g, SIDE * z + wrap(x + d))

    def Z(d):
        return (g, SIDE * wrap(z + d) + x)

    def Y(d):
        return (2 * wrap(y + d) + c, t)

    partner = (2 * y + (1 - c), t)

    sends = []
    count = [0]

    def new_sem():
        count[0] += 1
        return count[0] - 1

    def remote(src, dst, device):
        i = new_sem()
        copy = pltpu.make_async_remote_copy(
            src_ref=src, dst_ref=dst, send_sem=ssem.at[i], recv_sem=rsem.at[i],
            device_id=device, device_id_type=MESH,
        )
        copy.start()
        sends.append(copy)
        return copy

    def arrive(copies):
        for copy in copies:
            copy.wait_recv()

    barrier = pltpu.get_barrier_semaphore()
    peers = [
        (g, SIDE * wrap(z + dz) + wrap(x + dx)) for dz in range(SIDE) for dx in range(SIDE) if dz or dx
    ]
    peers += [Y(d) for d in range(1, SIDE)] + [partner]
    for peer in peers:
        pl.semaphore_signal(barrier, 1, device_id=peer, device_id_type=MESH)
    pl.semaphore_wait(barrier, len(peers))

    def spread(src_of, dst_of):
        first = [new_sem() for _ in range(SIDE)]
        out = []
        for d in range(1, SIDE):
            zz = wrap(z + d)
            out.append(
                pltpu.make_async_remote_copy(
                    src_ref=src_of(zz), dst_ref=dst_of(zz), send_sem=ssem.at[first[d]],
                    recv_sem=rsem.at[first[0]], device_id=Z(d), device_id_type=MESH,
                )
            )
        return out

    spread_in = spread(
        lambda zz: w_in.at[pl.ds(pl.multiple_of(c * EH + zz * ER, 16), ER), :],
        lambda zz: slab_in.at[zz, x],
    )

    spread_out = spread(
        lambda zz: w_out.at[
            pl.ds(pl.multiple_of(zz * OR, 16), OR), pl.ds(pl.multiple_of(c * EH, 128), EH)
        ],
        lambda zz: slab_out.at[zz, x],
    )

    @pl.when(z == y)
    def _():
        for copy in spread_in + spread_out:
            copy.start()

    swap = []
    for src, dst in ((w_gate, raw_g), (w_up, raw_u), (w_down, raw_d)):
        swap.append(remote(src, dst.at[c], partner))

    @pl.when(z == y)
    def _():
        slab_in[z, x] = w_in[pl.ds(pl.multiple_of(c * EH + z * ER, 16), ER), :]
        piece = w_out[pl.ds(pl.multiple_of(z * OR, 16), OR), :]
        slab_out[z, x] = jnp.where(c == 0, piece[:, :EH], piece[:, EH:])

    for src, dst in ((w_gate, raw_g), (w_up, raw_u), (w_down, raw_d)):
        dst[c] = src[...]

    bytes_here = states.shape[0]
    member = patch_row[...] == lax.broadcasted_iota(jnp.int32, (SLOTS, bytes_here), 0)
    member_bf = member.astype(BF)
    divisor = jnp.maximum(jnp.sum(member.astype(F32), axis=1, keepdims=True), 1.0)
    member_t = patch_col[...] == lax.broadcasted_iota(jnp.int32, (bytes_here, SLOTS), 1)
    member_t_bf = member_t.astype(BF)
    divisor_row = jnp.maximum(jnp.sum(member_t.astype(F32), axis=0, keepdims=True), 1.0)
    byte_divisor = jnp.sum(jnp.where(member_t, divisor_row, 0.0), axis=1, keepdims=True)
    pool[z, x] = (nn(member_bf, states[...]) / divisor).astype(BF)

    def gather_1(buf, cut):
        a = buf.at[(z, x) + cut(0)]
        b = buf.at[(z, x) + cut(1)]
        first = [remote(a, a, X(d)) for d in range(1, SIDE)]
        second = [remote(b, b, Z(d)) for d in range(1, SIDE)]
        return first, second

    def gather_2(buf, cut, one):
        arrive(one[0])
        a = buf.at[(z, slice(None)) + cut(0)]
        first = [remote(a, a, Z(d)) for d in range(1, SIDE)]
        arrive(one[1])
        b = buf.at[(slice(None), x) + cut(1)]
        second = [remote(b, b, X(d)) for d in range(1, SIDE)]
        return first + second

    def cut_rows(rows):
        return lambda h: (slice(h * rows // 2, (h + 1) * rows // 2), slice(None))

    def cut_cols(h):
        return (slice(None), slice(h * EH, (h + 1) * EH))

    def spread_arrive(copies):
        @pl.when(z != y)
        def _():
            copies[0].wait_recv()

    spread_arrive(spread_in)
    in_1 = gather_1(slab_in, cut_rows(ER))
    pool_1 = gather_1(pool, cut_cols)
    in_2 = gather_2(slab_in, cut_rows(ER), in_1)
    spread_arrive(spread_out)
    out_1 = gather_1(slab_out, cut_rows(OR))
    pool_2 = gather_2(pool, cut_cols, pool_1)
    out_2 = gather_2(slab_out, cut_rows(OR), out_1)
    arrive(swap)
    arrive(in_2)

    def block_in(raw):
        def f(b):
            total = jnp.zeros((ER, FB), F32)
            for xx in range(SIDE):
                lo = (xx % 2) * DT
                total += nn(slab_in[b, xx], raw[xx // 2, lo:lo + DT, :])
            return total
        return f

    def block_down(b):
        rows = pl.ds(pl.multiple_of(b * FR, 16), FR)
        total = jnp.zeros((FR, EH), F32)
        for xx in range(SIDE):
            lo = (xx % 2) * DT
            total += nn(raw_d[xx // 2, rows, lo:lo + DT], slab_out[:, xx].reshape(DT, EH))
        return total

    class Fold:
        def __init__(self, block, part, edge, mid, out, split):
            self.block, self.part, self.edge, self.mid, self.out, self.split = block, part, edge, mid, out, split

        def step_1(self):
            self.part[2] = self.block(wrap(y + 2)).astype(BF)
            s = self.split
            self.one = [
                remote(self.part.at[2, :s], self.edge.at[0, :s], Y(1)),
                remote(self.part.at[2, s:], self.edge.at[1, s:], Y(3)),
            ]

        def compute(self):
            for d in (1, 3, 0):
                self.part[d] = self.block(wrap(y + d)).astype(BF)

        def step_2(self):
            s = self.split
            self.one[0].wait_recv()
            self.part[1, :s] = (self.part[1, :s].astype(F32) + self.edge[0, :s].astype(F32)).astype(BF)
            two = [remote(self.part.at[1], self.mid.at[0], Y(1))]
            self.one[1].wait_recv()
            self.part[3, s:] = (self.part[3, s:].astype(F32) + self.edge[1, s:].astype(F32)).astype(BF)
            self.two = two + [remote(self.part.at[3], self.mid.at[1], Y(3))]

        def step_3(self):
            arrive(self.two)
            total = self.part[0].astype(F32) + self.mid[0].astype(F32) + self.mid[1].astype(F32)
            self.out[c, y] = total.astype(BF)
            own = self.out.at[c, y]
            self.three = [remote(own, own, Y(1)), remote(own, own, Y(3))]
            self.cross = [remote(own, own, partner)]

        def step_4(self):
            s = self.split
            self.three[0].wait_recv()
            low = self.out.at[c, wrap(y + 3)]
            four = [remote(low.at[:s], low.at[:s], Y(1))]
            self.cross.append(remote(low, low, partner))
            self.three[1].wait_recv()
            high = self.out.at[c, wrap(y + 1)]
            four.append(remote(high.at[s:], high.at[s:], Y(3)))
            self.cross.append(remote(high, high, partner))
            self.four = four

        def step_5(self):
            arrive(self.four)
            far = self.out.at[c, wrap(y + 2)]
            self.cross.append(remote(far, far, partner))
            arrive(self.cross)

    gate_f = Fold(block_in(raw_g), part_g, edge_g, mid_g, fold_g, ER // 2)
    up_f = Fold(block_in(raw_u), part_u, edge_u, mid_u, fold_u, ER // 2)
    down_f = Fold(block_down, part_d, edge_d, mid_d, fold_d, 64)

    gate_f.step_1()
    up_f.step_1()
    gate_f.compute()
    up_f.compute()
    gate_f.step_2()
    up_f.step_2()
    arrive(out_2)
    down_f.step_1()
    gate_f.step_3()
    up_f.step_3()
    down_f.compute()
    gate_f.step_4()
    up_f.step_4()
    down_f.step_2()
    gate_f.step_5()
    up_f.step_5()
    down_f.step_3()
    arrive(pool_2)

    def forward(i, carry):
        rows = pool[i].reshape(ROWS, E)
        act[i] = nn(rows, w_in[...]).astype(BF)
        gate_pre = nn(rows, fold_g[...].reshape(E, FB))
        up_pre = nn(rows, fold_u[...].reshape(E, FB))
        s = 1.0 / (1.0 + jnp.exp(-gate_pre))
        silu = gate_pre * s
        hid[i] = (silu * up_pre).astype(BF)
        gate_c[i] = up_pre * s * (1.0 + gate_pre * (1.0 - s))
        up_c[i] = silu
        return carry

    lax.fori_loop(0, 2, forward, 0)
    down_f.step_4()
    lax.fori_loop(2, SIDE, forward, 0)
    down_f.step_5()

    def scatter_sum(k, fill, buf):
        one_a, one_b = [], []
        for d in (1, 2, 3, 0):
            i = wrap(z + d)
            fill(i, 0)
            if d:
                one_a.append(remote(buf.at[i, :, :, :EH], rs1.at[k, 0, d - 1], Z(d)))
        for i in range(SIDE):
            fill(i, 1)
        for d in range(1, SIDE):
            one_b.append(remote(buf.at[:, wrap(x + d), :, EH:], rs1.at[k, 1, d - 1], X(d)))
        two_a, two_b = [], []
        for copy in one_a:
            copy.wait_recv()
        total = buf[z, :, :, :EH].astype(F32)
        for d in range(SIDE - 1):
            total += rs1[k, 0, d].astype(F32)
        mid1[k, 0] = total.astype(BF)
        for d in range(1, SIDE):
            two_a.append(remote(mid1.at[k, 0, wrap(x + d)], rs2.at[k, 0, d - 1], X(d)))
        for copy in one_b:
            copy.wait_recv()
        total = buf[:, x, :, EH:].astype(F32)
        for d in range(SIDE - 1):
            total += rs1[k, 1, d].astype(F32)
        mid1[k, 1] = total.astype(BF)
        for d in range(1, SIDE):
            two_b.append(remote(mid1.at[k, 1, wrap(z + d)], rs2.at[k, 1, d - 1], Z(d)))
        halves = []
        for h, (two, at) in enumerate(((two_a, x), (two_b, z))):
            arrive(two)
            total = mid1[k, h, at].astype(F32)
            for d in range(SIDE - 1):
                total += rs2[k, h, d].astype(F32)
            halves.append(total.astype(BF))
        return jnp.concatenate(halves, axis=1)

    def fill_out(i, h):
        term = nn(hid[i], fold_d[h].reshape(FB, EH)) + nn(act[i], w_out[:, h * EH:(h + 1) * EH])
        pout[i, :, :, h * EH:(h + 1) * EH] = term.astype(BF).reshape(SIDE, SLOTS, EH)

    patch_out = scatter_sum(0, fill_out, pout)

    decoder_in = states[...].astype(F32) + nn(member_t_bf, patch_out)
    inverse = lax.rsqrt(jnp.mean(decoder_in * decoder_in, axis=1, keepdims=True) + 1e-06)
    normal_part = decoder_in * inverse
    normed = (normal_part * gain[...]).astype(BF)
    logits = nn(normed, w_head[...])
    log_total = jnp.log(jnp.sum(jnp.exp(logits), axis=1, keepdims=True))
    is_target = targets[...] == lax.broadcasted_iota(jnp.int32, logits.shape, 1)
    chosen = jnp.sum(jnp.where(is_target, logits, 0.0), axis=1, keepdims=True)
    log_probs[...] = chosen - log_total
    probs = jnp.exp(logits - log_total)
    logit_grads = (cotangent[...] * (is_target.astype(F32) - probs)).astype(BF)
    scaled = nt(logit_grads, w_head[...]) * gain[...]
    decoder_grads = inverse * (
        scaled - normal_part * jnp.mean(scaled * normal_part, axis=1, keepdims=True)
    )
    high = decoder_grads.astype(BF)
    low = (decoder_grads - high.astype(F32)).astype(BF)
    grads[z, x] = (nn(member_bf, high) + nn(member_bf, low)).astype(BF)
    state_grads[...] = decoder_grads

    grads_1 = gather_1(grads, cut_cols)
    arrive(gather_2(grads, cut_cols, grads_1))

    def backward(i, carry):
        rows = grads[i].reshape(ROWS, E)
        hidden_grads = nt(rows[:, :EH], fold_d[0].reshape(FB, EH)) + nt(rows[:, EH:], fold_d[1].reshape(FB, EH))
        g_gate[i] = (hidden_grads * gate_c[i]).astype(BF)
        g_up[i] = (hidden_grads * up_c[i]).astype(BF)
        g_mix[i] = nt(rows, w_out[...]).astype(BF)
        return carry

    lax.fori_loop(0, SIDE, backward, 0)

    def fill_grads(i, h):
        term = (
            nt(g_gate[i], fold_g[h].reshape(EH, FB))
            + nt(g_up[i], fold_u[h].reshape(EH, FB))
            + nt(g_mix[i], w_in[h * EH:(h + 1) * EH, :])
        )
        qout[i, :, :, h * EH:(h + 1) * EH] = term.astype(BF).reshape(SIDE, SLOTS, EH)

    pooled_grads = scatter_sum(1, fill_grads, qout)
    state_grads[...] += nn(member_t_bf, pooled_grads) / byte_divisor

    @pl.when(z == y)
    def _():
        for copy in spread_in + spread_out:
            copy.wait_send()

    for copy in sends:
        copy.wait_send()


def body(
    states, patch_of, targets, cotangent, w_in, w_gate, w_up, w_down, w_out, head_gain, w_head
):
    n, E = states.shape
    DT = w_in.shape[1]
    DG, FB = w_gate.shape
    EH = E // 2
    ER, FR, OR = EH // SIDE, FB // SIDE, DT // SIDE
    ROWS = SIDE * SLOTS
    vmem = lambda *shape: pltpu.VMEM(shape, BF)
    vmem32 = lambda *shape: pltpu.VMEM(shape, F32)
    scratch = [
        vmem(2, DG, FB), vmem(2, DG, FB), vmem(2, FB, DG),
        vmem(SIDE, SIDE, ER, DT), vmem(SIDE, SIDE, OR, EH),
        vmem(SIDE, SIDE, SLOTS, E),
        vmem(2, SIDE, ER, FB), vmem(2, SIDE, ER, FB), vmem(2, SIDE, FR, EH),
        vmem(SIDE, ER, FB), vmem(SIDE, ER, FB), vmem(SIDE, FR, EH),
        vmem(2, ER, FB), vmem(2, ER, FB), vmem(2, FR, EH),
        vmem(2, ER, FB), vmem(2, ER, FB), vmem(2, FR, EH),
        vmem(SIDE, ROWS, DT),
        vmem32(SIDE, ROWS, FB), vmem32(SIDE, ROWS, FB),
        vmem(SIDE, ROWS, FB),
        vmem(SIDE, SIDE, SLOTS, E), vmem(SIDE, SIDE, SLOTS, E),
        vmem(SIDE, ROWS, FB), vmem(SIDE, ROWS, FB), vmem(SIDE, ROWS, DT),
        vmem(SIDE, SIDE, SLOTS, E),
        vmem(2, 2, SIDE - 1, SIDE, SLOTS, EH), vmem(2, 2, SIDE - 1, SLOTS, EH),
        vmem(2, 2, SIDE, SLOTS, EH),
        pltpu.SemaphoreType.DMA((N_SEMS,)), pltpu.SemaphoreType.DMA((N_SEMS,)),
    ]
    spec = pl.BlockSpec(memory_space=pltpu.VMEM)
    log_probs, state_grads = pl.pallas_call(
        kernel,
        out_shape=(jax.ShapeDtypeStruct((n, 1), F32), jax.ShapeDtypeStruct((n, E), F32)),
        in_specs=[spec] * 12,
        out_specs=(spec, spec),
        scratch_shapes=scratch,
        compiler_params=pltpu.CompilerParams(
            collective_id=0, has_side_effects=True, vmem_limit_bytes=60 * 2**20
        ),
        name="patch_step",
    )(
        states, patch_of.reshape(1, n), patch_of.reshape(n, 1), targets.reshape(n, 1), cotangent.reshape(n, 1),
        w_in, w_gate, w_up, w_down, w_out, head_gain.reshape(1, E), w_head,
    )
    return log_probs.reshape(n), state_grads


def solution(mesh):
    return jax.shard_map(
        body,
        mesh=mesh,
        in_specs=(
            P(("grp", "tp"), None),
            P(("grp", "tp")),
            P(("grp", "tp")),
            P(("grp", "tp")),
            P(None, "tp"),
            P("grp", "tp"),
            P("grp", "tp"),
            P("tp", "grp"),
            P("tp", None),
            P(),
            P(),
        ),
        out_specs=(P(("grp", "tp")), P(("grp", "tp"), None)),
        check_vma=False,
    )
```

```python
import jax
import jax.numpy as jnp
from jax import lax
from jax.experimental import pallas as pl
from jax.experimental.pallas import tpu as pltpu
from jax.sharding import PartitionSpec as P

BF = jnp.bfloat16
F32 = jnp.float32
MESH = pl.DeviceIdType.MESH
SIDE = 4
SLOTS = 48
N_SEMS = 288


def nn(a, b):
    return lax.dot_general(a, b, (((1,), (0,)), ((), ())), preferred_element_type=F32)


def nt(a, b):
    return lax.dot_general(a, b, (((1,), (1,)), ((), ())), preferred_element_type=F32)


def wrap(v):
    return lax.rem(v, SIDE)


def kernel(
    states, patch_of, targets, cotangent, w_in, w_gate, w_up, w_down, w_out, gain, w_head,
    log_probs, state_grads,
    raw_g, raw_u, raw_d, head_w, slab_in, slab_out, pool, fold_g, fold_u, fold_d,
    part_g, part_u, part_d, edge_g, edge_u, edge_d, mid_g, mid_u, mid_d,
    act, gate_c, up_c, hid, pout, qout, g_gate, g_up, g_mix, grads,
    rs1, rs2, mid1,
    ssem, rsem, lsem,
):
    N, E = states.shape
    EH = E // 2
    FB = w_gate.shape[0]
    DT = w_in.shape[1]
    ER = EH // SIDE
    FR = FB // SIDE
    OR = DT // SIDE
    ROWS = SIDE * SLOTS

    g = lax.axis_index("grp")
    t = lax.axis_index("tp")
    y, c = g // 2, g % 2
    z, x = t // SIDE, t % SIDE

    def X(d):
        return (g, SIDE * z + wrap(x + d))

    def Z(d):
        return (g, SIDE * wrap(z + d) + x)

    def Y(d):
        return (2 * wrap(y + d) + c, t)

    partner = (2 * y + (1 - c), t)

    sends = []
    count = [0]

    def new_sem():
        count[0] += 1
        return count[0] - 1

    def remote(src, dst, device):
        i = new_sem()
        copy = pltpu.make_async_remote_copy(
            src_ref=src, dst_ref=dst, send_sem=ssem.at[i], recv_sem=rsem.at[i],
            device_id=device, device_id_type=MESH,
        )
        copy.start()
        sends.append(copy)
        return copy

    def arrive(copies):
        for copy in copies:
            copy.wait_recv()

    barrier = pltpu.get_barrier_semaphore()
    peers = [X(d) for d in (1, 2, 3)] + [Z(d) for d in (1, 2, 3)] + [Y(1), Y(3), partner]
    for peer in peers:
        pl.semaphore_signal(barrier, 1, device_id=peer, device_id_type=MESH)

    local = [
        pltpu.make_async_copy(src, dst, lsem.at[i])
        for i, (src, dst) in enumerate(
            ((w_gate, raw_g.at[c]), (w_up, raw_u.at[c]), (w_down, raw_d.at[c]), (w_head, head_w))
        )
    ]
    for copy in local:
        copy.start()

    def column(row):
        return jnp.transpose(jnp.broadcast_to(row, (N, N)))[:, :1]

    member = patch_of[...] == lax.broadcasted_iota(jnp.int32, (SLOTS, N), 0)
    member_bf = member.astype(BF)
    divisor = jnp.maximum(jnp.sum(member.astype(F32), axis=1, keepdims=True), 1.0)
    pool[z, x] = (nn(member_bf, states[...]) / divisor).astype(BF)

    pl.semaphore_wait(barrier, len(peers))

    def spread(src_of, dst_of):
        first = [new_sem() for _ in range(SIDE)]
        out = []
        for d in range(1, SIDE):
            zz = wrap(z + d)
            out.append(
                pltpu.make_async_remote_copy(
                    src_ref=src_of(zz), dst_ref=dst_of(zz), send_sem=ssem.at[first[d]],
                    recv_sem=rsem.at[first[0]], device_id=Z(d), device_id_type=MESH,
                )
            )
        return out

    spread_in = spread(
        lambda zz: w_in.at[pl.ds(pl.multiple_of(c * EH + zz * ER, 16), ER), :],
        lambda zz: slab_in.at[zz, x],
    )

    spread_out = spread(
        lambda zz: w_out.at[
            pl.ds(pl.multiple_of(zz * OR, 16), OR), pl.ds(pl.multiple_of(c * EH, 128), EH)
        ],
        lambda zz: slab_out.at[zz, x],
    )

    def spread_start(copies):
        @pl.when(z == y)
        def _():
            for copy in copies:
                copy.start()

    def spread_arrive(copies):
        @pl.when(z != y)
        def _():
            copies[0].wait_recv()

    spread_start(spread_in)

    swap = []
    for src, dst in ((w_gate, raw_g), (w_up, raw_u), (w_down, raw_d)):
        swap.append(remote(src, dst.at[c], partner))

    @pl.when(z == y)
    def _():
        slab_in[z, x] = w_in[pl.ds(pl.multiple_of(c * EH + z * ER, 16), ER), :]
        piece = w_out[pl.ds(pl.multiple_of(z * OR, 16), OR), :]
        slab_out[z, x] = jnp.where(c == 0, piece[:, :EH], piece[:, EH:])

    def gather(buf, cut):
        def slot(h, f, s, piece=None):
            at = (wrap(z + s + 4), wrap(x + f + 4)) if h == 0 else (wrap(z + f + 4), wrap(x + s + 4))
            return buf.at[at + cut(h, piece)]

        def first(h, d):
            return X(d % SIDE) if h == 0 else Z(d % SIDE)

        def second(h, d):
            return Z(d % SIDE) if h == 0 else X(d % SIDE)

        def send(ref, device):
            return remote(ref, ref, device)

        one, two, far, last = {}, {}, {}, []
        for h in range(2):
            for d in (1, -1):
                one[h, d] = send(slot(h, 0, 0), first(h, d))
        for h in range(2):
            for d in (1, -1):
                two[h, 0, d] = send(slot(h, 0, 0), second(h, d))
        yield
        for d in (1, -1):
            for h in range(2):
                one[h, d].wait_recv()
                far[h, d] = send(slot(h, -d, 0, (1 - d) // 2), first(h, d))
                for e in (1, -1):
                    two[h, -d, e] = send(slot(h, -d, 0), second(h, e))
        yield

        def onward(f):
            for d in (1, -1):
                for h in range(2):
                    two[h, f, d].wait_recv()
                    last.append(send(slot(h, f, -d, (1 - d) // 2), second(h, d)))

        onward(0)
        yield
        for h in range(2):
            far[h, 1].wait_recv()
            far[h, -1].wait_recv()
            for e in (1, -1):
                two[h, 2, e] = send(slot(h, 2, 0), second(h, e))
        yield
        onward(-1)
        onward(1)
        yield
        onward(2)
        yield
        arrive(last)

    def cut_rows(rows, split):
        def cut(h, piece):
            lo, hi = h * rows // 2, (h + 1) * rows // 2
            mid = lo + split[h]
            if piece == 0:
                hi = mid
            elif piece == 1:
                lo = mid
            return (slice(lo, hi), slice(None))
        return cut

    def cut_cols(h, piece):
        lo, hi = h * EH, (h + 1) * EH
        mid = lo + (384 if h == 0 else 256)
        if piece == 0:
            hi = mid
        elif piece == 1:
            lo = mid
        return (slice(None), slice(lo, hi))

    def run(gen):
        for _ in gen:
            pass

    in_g = gather(slab_in, cut_rows(ER, (48, 32)))
    out_g = gather(slab_out, cut_rows(OR, (16, 16)))
    pool_g = gather(pool, cut_cols)

    spread_arrive(spread_in)
    next(in_g)
    next(pool_g)
    for _ in range(4):
        next(in_g)
    spread_start(spread_out)
    run(in_g)
    arrive(swap[:2])
    for copy in local[:2]:
        copy.wait()

    def block_in(raw):
        def f(b):
            total = jnp.zeros((ER, FB), F32)
            for xx in range(SIDE):
                lo = (xx % 2) * DT
                total += nt(slab_in[b, xx], raw[xx // 2, :, lo:lo + DT])
            return total
        return f

    def block_down(b):
        rows = pl.ds(pl.multiple_of(b * FR, 16), FR)
        total = jnp.zeros((FR, EH), F32)
        for xx in range(SIDE):
            lo = (xx % 2) * DT
            total += nn(raw_d[xx // 2, rows, lo:lo + DT], slab_out[:, xx].reshape(DT, EH))
        return total

    class Fold:
        def __init__(self, block, part, edge, mid, out, split):
            self.block, self.part, self.edge, self.mid, self.out, self.split = block, part, edge, mid, out, split

        def step_1(self):
            self.part[2] = self.block(wrap(y + 2)).astype(BF)
            s = self.split
            self.one = [
                remote(self.part.at[2, :s], self.edge.at[0, :s], Y(1)),
                remote(self.part.at[2, s:], self.edge.at[1, s:], Y(3)),
            ]

        def compute(self):
            for d in (1, 3, 0):
                self.part[d] = self.block(wrap(y + d)).astype(BF)

        def step_2(self):
            s = self.split
            self.one[0].wait_recv()
            self.part[1, :s] = (self.part[1, :s].astype(F32) + self.edge[0, :s].astype(F32)).astype(BF)
            two = [remote(self.part.at[1], self.mid.at[0], Y(1))]
            self.one[1].wait_recv()
            self.part[3, s:] = (self.part[3, s:].astype(F32) + self.edge[1, s:].astype(F32)).astype(BF)
            self.two = two + [remote(self.part.at[3], self.mid.at[1], Y(3))]

        def step_3(self):
            arrive(self.two)
            total = self.part[0].astype(F32) + self.mid[0].astype(F32) + self.mid[1].astype(F32)
            self.out[c, y] = total.astype(BF)
            own = self.out.at[c, y]
            self.three = [remote(own, own, Y(1)), remote(own, own, Y(3))]
            self.cross = [remote(own, own, partner)]

        def step_4(self):
            s = self.split
            self.three[0].wait_recv()
            low = self.out.at[c, wrap(y + 3)]
            four = [remote(low.at[:s], low.at[:s], Y(1))]
            self.cross.append(remote(low, low, partner))
            self.three[1].wait_recv()
            high = self.out.at[c, wrap(y + 1)]
            four.append(remote(high.at[s:], high.at[s:], Y(3)))
            self.cross.append(remote(high, high, partner))
            self.four = four

        def step_5(self):
            arrive(self.four)
            far = self.out.at[c, wrap(y + 2)]
            self.cross.append(remote(far, far, partner))
            arrive(self.cross)

    gate_f = Fold(block_in(raw_g), part_g, edge_g, mid_g, fold_g, ER // 2)
    up_f = Fold(block_in(raw_u), part_u, edge_u, mid_u, fold_u, ER // 2)
    down_f = Fold(block_down, part_d, edge_d, mid_d, fold_d, 64)

    gate_f.step_1()
    up_f.step_1()
    next(pool_g)
    gate_f.compute()
    up_f.compute()
    gate_f.step_2()
    spread_arrive(spread_out)
    next(out_g)
    up_f.step_2()
    next(pool_g)
    next(out_g)
    gate_f.step_3()
    next(out_g)
    next(pool_g)
    up_f.step_3()
    next(out_g)
    next(pool_g)
    gate_f.step_4()
    next(out_g)
    next(out_g)
    next(pool_g)
    up_f.step_4()
    run(out_g)
    arrive(swap[2:])
    local[2].wait()
    down_f.step_1()
    down_f.compute()
    run(pool_g)
    gate_f.step_5()
    up_f.step_5()

    def forward(i, carry):
        rows = pool[i].reshape(ROWS, E)
        act[i] = nn(rows, w_in[...]).astype(BF)
        gate_pre = nn(rows, fold_g[...].reshape(E, FB))
        up_pre = nn(rows, fold_u[...].reshape(E, FB))
        s = 1.0 / (1.0 + jnp.exp(-gate_pre))
        silu = gate_pre * s
        hid[i] = (silu * up_pre).astype(BF)
        gate_c[i] = up_pre * s * (1.0 + gate_pre * (1.0 - s))
        up_c[i] = silu
        return carry

    lax.fori_loop(0, 2, forward, 0)
    down_f.step_2()
    lax.fori_loop(2, SIDE, forward, 0)
    down_f.step_3()
    down_f.step_4()
    down_f.step_5()

    def scatter_sum(k, fill, buf):
        one, two = {}, {}

        def cols(h):
            return slice(h * EH, (h + 1) * EH)

        def send_one(h, q):
            for p in (1, 3, 2):
                at = (wrap(z + p), wrap(x + q)) if h == 0 else (wrap(z + q), wrap(x + p))
                one[h, q, p] = remote(
                    buf.at[at + (slice(None), cols(h))], rs1.at[k, h, p - 1, q], Z(p) if h == 0 else X(p)
                )

        fill(wrap(z + 2), 1)
        send_one(1, 2)
        for d in (1, 3, 2):
            fill(wrap(z + d), 0)
        for q in (2, 1, 3, 0):
            send_one(0, q)
        for q in (1, 3, 0):
            fill(wrap(z + q), 1)
            send_one(1, q)
        fill(z, 0)
        halves = {}
        for q in (2, 1, 3, 0):
            for h in (1, 0):
                at = (z, wrap(x + q)) if h == 0 else (wrap(z + q), x)
                for p in (1, 3, 2):
                    one[h, q, p].wait_recv()
                total = buf[at + (slice(None), cols(h))].astype(F32)
                for p in range(SIDE - 1):
                    total += rs1[k, h, p, q].astype(F32)
                if q:
                    mid1[k, h, q] = total.astype(BF)
                    two[h, q] = remote(
                        mid1.at[k, h, q], rs2.at[k, h, q - 1], X(q) if h == 0 else Z(q)
                    )
                else:
                    halves[h] = total
        for h in range(2):
            total = halves[h]
            for q in (1, 3, 2):
                two[h, q].wait_recv()
                total += rs2[k, h, q - 1].astype(F32)
            halves[h] = total.astype(BF)
        return jnp.concatenate([halves[0], halves[1]], axis=1)

    def fill_out(i, h):
        term = nn(hid[i], fold_d[h].reshape(FB, EH)) + nn(act[i], w_out[:, h * EH:(h + 1) * EH])
        pout[i, :, :, h * EH:(h + 1) * EH] = term.astype(BF).reshape(SIDE, SLOTS, EH)

    patch_out = scatter_sum(0, fill_out, pout)

    patch_col = column(patch_of[...])
    member_t = patch_col == lax.broadcasted_iota(jnp.int32, (N, SLOTS), 1)
    member_t_bf = member_t.astype(BF)
    decoder_in = states[...].astype(F32) + nn(member_t_bf, patch_out)
    inverse = lax.rsqrt(jnp.mean(decoder_in * decoder_in, axis=1, keepdims=True) + 1e-06)
    normal_part = decoder_in * inverse
    gains = gain[...].reshape(1, E)
    normed = (normal_part * gains).astype(BF)
    local[3].wait()
    logits = nn(normed, head_w[...])
    log_total = jnp.log(jnp.sum(jnp.exp(logits), axis=1, keepdims=True))
    is_target = column(targets[...]) == lax.broadcasted_iota(jnp.int32, logits.shape, 1)
    chosen = jnp.sum(jnp.where(is_target, logits, 0.0), axis=1, keepdims=True)
    log_probs[...] = jnp.transpose(jnp.broadcast_to(chosen - log_total, (N, N)))[:1, :]
    probs = jnp.exp(logits - log_total)
    logit_grads = (column(cotangent[...]) * (is_target.astype(F32) - probs)).astype(BF)
    scaled = nt(logit_grads, head_w[...]) * gains
    decoder_grads = inverse * (
        scaled - normal_part * jnp.mean(scaled * normal_part, axis=1, keepdims=True)
    )
    high = decoder_grads.astype(BF)
    low = (decoder_grads - high.astype(F32)).astype(BF)
    grads[z, x] = (nn(member_bf, high) + nn(member_bf, low)).astype(BF)

    grads_g = gather(grads, cut_cols)
    next(grads_g)
    state_grads[...] = decoder_grads
    run(grads_g)

    def backward(i, carry):
        rows = grads[i].reshape(ROWS, E)
        hidden_grads = nt(rows[:, :EH], fold_d[0].reshape(FB, EH)) + nt(rows[:, EH:], fold_d[1].reshape(FB, EH))
        g_gate[i] = (hidden_grads * gate_c[i]).astype(BF)
        g_up[i] = (hidden_grads * up_c[i]).astype(BF)
        g_mix[i] = nt(rows, w_out[...]).astype(BF)
        return carry

    lax.fori_loop(0, SIDE, backward, 0)

    def fill_grads(i, h):
        term = (
            nt(g_gate[i], fold_g[h].reshape(EH, FB))
            + nt(g_up[i], fold_u[h].reshape(EH, FB))
            + nt(g_mix[i], w_in[h * EH:(h + 1) * EH, :])
        )
        qout[i, :, :, h * EH:(h + 1) * EH] = term.astype(BF).reshape(SIDE, SLOTS, EH)

    pooled_grads = scatter_sum(1, fill_grads, qout)
    divisor_row = jnp.maximum(jnp.sum(member_t.astype(F32), axis=0, keepdims=True), 1.0)
    byte_divisor = jnp.sum(jnp.where(member_t, divisor_row, 0.0), axis=1, keepdims=True)
    state_grads[...] += nn(member_t_bf, pooled_grads) / byte_divisor

    @pl.when(z == y)
    def _():
        for copy in spread_in + spread_out:
            copy.wait_send()

    for copy in sends:
        copy.wait_send()


def body(
    states, patch_of, targets, cotangent, w_in, w_gate, w_up, w_down, w_out, head_gain, w_head
):
    n, E = states.shape
    DT = w_in.shape[1]
    DG, FB = w_gate.shape
    V = w_head.shape[1]
    EH = E // 2
    ER, FR, OR = EH // SIDE, FB // SIDE, DT // SIDE
    ROWS = SIDE * SLOTS
    vmem = lambda *shape: pltpu.VMEM(shape, BF)
    vmem32 = lambda *shape: pltpu.VMEM(shape, F32)
    scratch = [
        vmem(2, FB, DG), vmem(2, FB, DG), vmem(2, FB, DG), vmem(E, V),
        vmem(SIDE, SIDE, ER, DT), vmem(SIDE, SIDE, OR, EH),
        vmem(SIDE, SIDE, SLOTS, E),
        vmem(2, SIDE, ER, FB), vmem(2, SIDE, ER, FB), vmem(2, SIDE, FR, EH),
        vmem(SIDE, ER, FB), vmem(SIDE, ER, FB), vmem(SIDE, FR, EH),
        vmem(2, ER, FB), vmem(2, ER, FB), vmem(2, FR, EH),
        vmem(2, ER, FB), vmem(2, ER, FB), vmem(2, FR, EH),
        vmem(SIDE, ROWS, DT),
        vmem32(SIDE, ROWS, FB), vmem32(SIDE, ROWS, FB),
        vmem(SIDE, ROWS, FB),
        vmem(SIDE, SIDE, SLOTS, E), vmem(SIDE, SIDE, SLOTS, E),
        vmem(SIDE, ROWS, FB), vmem(SIDE, ROWS, FB), vmem(SIDE, ROWS, DT),
        vmem(SIDE, SIDE, SLOTS, E),
        vmem(2, 2, SIDE - 1, SIDE, SLOTS, EH), vmem(2, 2, SIDE - 1, SLOTS, EH),
        vmem(2, 2, SIDE, SLOTS, EH),
        pltpu.SemaphoreType.DMA((N_SEMS,)), pltpu.SemaphoreType.DMA((N_SEMS,)),
        pltpu.SemaphoreType.DMA((4,)),
    ]
    near = pl.BlockSpec(memory_space=pltpu.VMEM)
    away = pl.BlockSpec(memory_space=pl.ANY)
    log_probs, state_grads = pl.pallas_call(
        kernel,
        out_shape=(jax.ShapeDtypeStruct((1, n), F32), jax.ShapeDtypeStruct((n, E), F32)),
        in_specs=[near] * 5 + [away] * 3 + [near] * 2 + [away],
        out_specs=(near, near),
        scratch_shapes=scratch,
        compiler_params=pltpu.CompilerParams(
            collective_id=0, has_side_effects=True, vmem_limit_bytes=60 * 2**20
        ),
        name="patch_step",
    )(
        states, patch_of.reshape(1, n), targets.reshape(1, n), cotangent.reshape(1, n),
        w_in, w_gate.T, w_up.T, w_down, w_out, head_gain, w_head,
    )
    return log_probs.reshape(n), state_grads


def solution(mesh):
    return jax.shard_map(
        body,
        mesh=mesh,
        in_specs=(
            P(("grp", "tp"), None),
            P(("grp", "tp")),
            P(("grp", "tp")),
            P(("grp", "tp")),
            P(None, "tp"),
            P("grp", "tp"),
            P("grp", "tp"),
            P("tp", "grp"),
            P("tp", None),
            P(),
            P(),
        ),
        out_specs=(P(("grp", "tp")), P(("grp", "tp"), None)),
        check_vma=False,
    )
```

```python
import jax
import jax.numpy as jnp
from jax import lax
from jax.experimental import pallas as pl
from jax.experimental.pallas import tpu as pltpu
from jax.sharding import PartitionSpec as P

BF = jnp.bfloat16
F32 = jnp.float32
MESH = pl.DeviceIdType.MESH
SIDE = 4
SLOTS = 48
N_SEMS = 256


def nn(a, b):
    return lax.dot_general(a, b, (((1,), (0,)), ((), ())), preferred_element_type=F32)


def nt(a, b):
    return lax.dot_general(a, b, (((1,), (1,)), ((), ())), preferred_element_type=F32)


def wrap(v):
    return lax.rem(v, SIDE)


def kernel(
    states, patch_of, targets, cotangent, w_in, w_gate, w_up, w_down, w_out, gain, w_head,
    log_probs, state_grads,
    raw_g, raw_u, raw_d, head_w, slab_in, slab_out, pool, fold_g, fold_u, fold_d,
    part_g, part_u, part_d, edge_g, edge_u, edge_d, mid_g, mid_u, mid_d,
    act, gate_c, up_c, hid, pout, qout, g_gate, g_up, g_mix, grads,
    rs1, rs2, mid1,
    ssem, rsem, lsem,
):
    N, E = states.shape
    EH = E // 2
    FB = w_gate.shape[0]
    DT = w_in.shape[1]
    ER = EH // SIDE
    FR = FB // SIDE
    OR = DT // SIDE
    ROWS = SIDE * SLOTS

    g = lax.axis_index("grp")
    t = lax.axis_index("tp")
    y, c = g // 2, g % 2
    z, x = t // SIDE, t % SIDE

    def X(d):
        return (g, SIDE * z + wrap(x + d))

    def Z(d):
        return (g, SIDE * wrap(z + d) + x)

    def Y(d):
        return (2 * wrap(y + d) + c, t)

    partner = (2 * y + (1 - c), t)

    sends = []
    count = [0]

    def new_sem():
        count[0] += 1
        return count[0] - 1

    def remote(src, dst, device):
        i = new_sem()
        copy = pltpu.make_async_remote_copy(
            src_ref=src, dst_ref=dst, send_sem=ssem.at[i], recv_sem=rsem.at[i],
            device_id=device, device_id_type=MESH,
        )
        copy.start()
        sends.append(copy)
        return copy

    def arrive(copies):
        for copy in copies:
            copy.wait_recv()

    barrier = pltpu.get_barrier_semaphore()
    peers = [X(d) for d in (1, 2, 3)] + [Z(d) for d in (1, 2, 3)] + [Y(1), Y(3), partner]
    for peer in peers:
        pl.semaphore_signal(barrier, 1, device_id=peer, device_id_type=MESH)

    local = [
        pltpu.make_async_copy(src, dst, lsem.at[i])
        for i, (src, dst) in enumerate(
            ((w_gate, raw_g.at[c]), (w_up, raw_u.at[c]), (w_down, raw_d.at[c]), (w_head, head_w))
        )
    ]
    for copy in local:
        copy.start()

    def column(row):
        return jnp.transpose(jnp.broadcast_to(row, (N, N)))[:, :1]

    member = patch_of[...] == lax.broadcasted_iota(jnp.int32, (SLOTS, N), 0)
    member_bf = member.astype(BF)
    divisor = jnp.maximum(jnp.sum(member.astype(F32), axis=1, keepdims=True), 1.0)
    pool[z, x] = (nn(member_bf, states[...]) / divisor).astype(BF)

    pl.semaphore_wait(barrier, len(peers))

    def spread(src_of, dst_of):
        first = [new_sem() for _ in range(SIDE)]
        out = []
        for d in range(1, SIDE):
            zz = wrap(z + d)
            out.append(
                pltpu.make_async_remote_copy(
                    src_ref=src_of(zz), dst_ref=dst_of(zz), send_sem=ssem.at[first[d]],
                    recv_sem=rsem.at[first[0]], device_id=Z(d), device_id_type=MESH,
                )
            )
        return out

    spread_in = spread(
        lambda zz: w_in.at[pl.ds(pl.multiple_of(c * EH + zz * ER, 16), ER), :],
        lambda zz: slab_in.at[zz, x],
    )

    spread_out = spread(
        lambda zz: w_out.at[
            pl.ds(pl.multiple_of(zz * OR, 16), OR), pl.ds(pl.multiple_of(c * EH, 128), EH)
        ],
        lambda zz: slab_out.at[zz, x],
    )

    def spread_start(copies):
        @pl.when(z == y)
        def _():
            for copy in copies:
                copy.start()

    def spread_arrive(copies):
        @pl.when(z != y)
        def _():
            copies[0].wait_recv()

    spread_start(spread_in)
    spread_start(spread_out)

    swap = []
    for src, dst in ((w_gate, raw_g), (w_up, raw_u), (w_down, raw_d)):
        swap.append(remote(src, dst.at[c], partner))

    @pl.when(z == y)
    def _():
        slab_in[z, x] = w_in[pl.ds(pl.multiple_of(c * EH + z * ER, 16), ER), :]
        piece = w_out[pl.ds(pl.multiple_of(z * OR, 16), OR), :]
        slab_out[z, x] = jnp.where(c == 0, piece[:, :EH], piece[:, EH:])

    def gather(buf, cut, ring):
        def slot(h, f, s, piece=None):
            at = (wrap(z + s + 4), wrap(x + f + 4)) if h == 0 else (wrap(z + f + 4), wrap(x + s + 4))
            return buf.at[at + cut(h, piece)]

        def first(h, d):
            return X(d) if h == 0 else Z(d)

        def second(h, d):
            return Z(d) if h == 0 else X(d)

        def send(ref, device):
            return remote(ref, ref, device)

        ways = (1, 3) if ring else (1, 3, 2)
        one, two, last = {}, {}, []
        for d in (1, 3, 2):
            for h in range(2):
                one[h, d] = send(slot(h, 0, 0), first(h, d))
        for e in ways:
            for h in range(2):
                two[h, 0, e] = send(slot(h, 0, 0), second(h, e))
        yield
        for d in (1, 3, 2):
            for h in range(2):
                one[h, d].wait_recv()
                for e in ways:
                    two[h, d, e] = send(slot(h, -d, 0), second(h, e))
        yield
        if ring:
            for d in (0, 1, 3, 2):
                for e in ways:
                    for h in range(2):
                        two[h, d, e].wait_recv()
                        last.append(send(slot(h, -d, -e, e // 2), second(h, e)))
                yield
            arrive(last)
        else:
            arrive(two.values())

    def cut_rows(rows, split):
        def cut(h, piece):
            lo, hi = h * rows // 2, (h + 1) * rows // 2
            mid = lo + split[h]
            if piece == 0:
                hi = mid
            elif piece == 1:
                lo = mid
            return (slice(lo, hi), slice(None))
        return cut

    def cut_cols(h, piece):
        lo, hi = h * EH, (h + 1) * EH
        mid = lo + (384 if h == 0 else 256)
        if piece == 0:
            hi = mid
        elif piece == 1:
            lo = mid
        return (slice(None), slice(lo, hi))

    def run(gen):
        for _ in gen:
            pass

    in_g = gather(slab_in, cut_rows(ER, (48, 32)), False)
    out_g = gather(slab_out, cut_rows(OR, (16, 16)), False)
    pool_g = gather(pool, cut_cols, True)

    spread_arrive(spread_in)
    next(in_g)
    next(in_g)
    spread_arrive(spread_out)
    next(out_g)
    run(in_g)
    arrive(swap[:2])
    for copy in local[:2]:
        copy.wait()

    def block_in(raw):
        def f():
            total = jnp.zeros((EH, FB), F32)
            for xx in range(SIDE):
                lo = (xx % 2) * DT
                total += nt(slab_in[:, xx].reshape(EH, DT), raw[xx // 2, :, lo:lo + DT])
            return total.astype(BF).reshape(SIDE, ER, FB)
        return f

    def block_down():
        total = jnp.zeros((FB, EH), F32)
        for xx in range(SIDE):
            lo = (xx % 2) * DT
            total += nn(raw_d[xx // 2, :, lo:lo + DT], slab_out[:, xx].reshape(DT, EH))
        return total.astype(BF).reshape(SIDE, FR, EH)

    class Fold:
        def __init__(self, block, part, edge, mid, out, split):
            self.block, self.part, self.edge, self.mid, self.out, self.split = block, part, edge, mid, out, split

        def step_1(self):
            self.part[...] = self.block()
            s = self.split
            far = wrap(y + 2)
            self.one = [
                remote(self.part.at[far, :s], self.edge.at[0, :s], Y(1)),
                remote(self.part.at[far, s:], self.edge.at[1, s:], Y(3)),
            ]

        def step_2(self):
            s = self.split
            right, left = wrap(y + 1), wrap(y + 3)
            self.one[0].wait_recv()
            self.part[right, :s] = (self.part[right, :s].astype(F32) + self.edge[0, :s].astype(F32)).astype(BF)
            two = [remote(self.part.at[right], self.mid.at[0], Y(1))]
            self.one[1].wait_recv()
            self.part[left, s:] = (self.part[left, s:].astype(F32) + self.edge[1, s:].astype(F32)).astype(BF)
            self.two = two + [remote(self.part.at[left], self.mid.at[1], Y(3))]

        def step_3(self):
            arrive(self.two)
            total = self.part[y].astype(F32) + self.mid[0].astype(F32) + self.mid[1].astype(F32)
            self.out[c, y] = total.astype(BF)
            own = self.out.at[c, y]
            self.three = [remote(own, own, Y(1)), remote(own, own, Y(3))]
            self.cross = [remote(own, own, partner)]

        def step_4(self):
            s = self.split
            self.three[0].wait_recv()
            low = self.out.at[c, wrap(y + 3)]
            four = [remote(low.at[:s], low.at[:s], Y(1))]
            self.cross.append(remote(low, low, partner))
            self.three[1].wait_recv()
            high = self.out.at[c, wrap(y + 1)]
            four.append(remote(high.at[s:], high.at[s:], Y(3)))
            self.cross.append(remote(high, high, partner))
            self.four = four

        def step_5(self):
            arrive(self.four)
            far = self.out.at[c, wrap(y + 2)]
            self.cross.append(remote(far, far, partner))
            arrive(self.cross)

    gate_f = Fold(block_in(raw_g), part_g, edge_g, mid_g, fold_g, ER // 2)
    up_f = Fold(block_in(raw_u), part_u, edge_u, mid_u, fold_u, ER // 2)
    down_f = Fold(block_down, part_d, edge_d, mid_d, fold_d, 64)

    gate_f.step_1()
    up_f.step_1()
    next(out_g)
    next(pool_g)
    gate_f.step_2()
    up_f.step_2()
    run(out_g)
    arrive(swap[2:])
    local[2].wait()
    down_f.step_1()
    next(pool_g)
    gate_f.step_3()
    up_f.step_3()
    down_f.step_2()
    next(pool_g)
    gate_f.step_4()
    up_f.step_4()
    next(pool_g)
    down_f.step_3()
    next(pool_g)
    gate_f.step_5()
    up_f.step_5()
    run(pool_g)

    def forward(i, carry):
        rows = pool[i].reshape(ROWS, E)
        act[i] = nn(rows, w_in[...]).astype(BF)
        gate_pre = nn(rows, fold_g[...].reshape(E, FB))
        up_pre = nn(rows, fold_u[...].reshape(E, FB))
        s = 1.0 / (1.0 + jnp.exp(-gate_pre))
        silu = gate_pre * s
        hid[i] = (silu * up_pre).astype(BF)
        gate_c[i] = up_pre * s * (1.0 + gate_pre * (1.0 - s))
        up_c[i] = silu
        return carry

    lax.fori_loop(0, 2, forward, 0)
    down_f.step_4()
    lax.fori_loop(2, SIDE, forward, 0)
    down_f.step_5()

    def scatter_sum(k, fill, buf):
        one, two = {}, {}

        def cols(h):
            return slice(h * EH, (h + 1) * EH)

        def send_one(h, p, q):
            at = (wrap(z + p), wrap(x + q)) if h == 0 else (wrap(z + q), wrap(x + p))
            one[h, q, p] = remote(
                buf.at[at + (slice(None), cols(h))], rs1.at[k, h, p - 1, q], Z(p) if h == 0 else X(p)
            )

        for d in (2, 1, 3, 0):
            fill(wrap(z + d), 0)
            if d:
                for q in (2, 1, 3, 0):
                    send_one(0, d, q)
            fill(wrap(z + d), 1)
            for p in (1, 3, 2):
                send_one(1, p, d)
        halves = {}
        for q in (2, 1, 3, 0):
            for h in (1, 0):
                at = (z, wrap(x + q)) if h == 0 else (wrap(z + q), x)
                for p in (1, 3, 2):
                    one[h, q, p].wait_recv()
                total = buf[at + (slice(None), cols(h))].astype(F32)
                for p in range(SIDE - 1):
                    total += rs1[k, h, p, q].astype(F32)
                if q:
                    mid1[k, h, q] = total.astype(BF)
                    two[h, q] = remote(
                        mid1.at[k, h, q], rs2.at[k, h, q - 1], X(q) if h == 0 else Z(q)
                    )
                else:
                    halves[h] = total
        for h in range(2):
            total = halves[h]
            for q in (1, 3, 2):
                two[h, q].wait_recv()
                total += rs2[k, h, q - 1].astype(F32)
            halves[h] = total.astype(BF)
        return jnp.concatenate([halves[0], halves[1]], axis=1)

    def fill_out(i, h):
        term = nn(hid[i], fold_d[h].reshape(FB, EH)) + nn(act[i], w_out[:, h * EH:(h + 1) * EH])
        pout[i, :, :, h * EH:(h + 1) * EH] = term.astype(BF).reshape(SIDE, SLOTS, EH)

    patch_out = scatter_sum(0, fill_out, pout)

    patch_col = column(patch_of[...])
    member_t = patch_col == lax.broadcasted_iota(jnp.int32, (N, SLOTS), 1)
    member_t_bf = member_t.astype(BF)
    decoder_in = states[...].astype(F32) + nn(member_t_bf, patch_out)
    inverse = lax.rsqrt(jnp.mean(decoder_in * decoder_in, axis=1, keepdims=True) + 1e-06)
    normal_part = decoder_in * inverse
    gains = gain[...].reshape(1, E)
    normed = (normal_part * gains).astype(BF)
    local[3].wait()
    logits = nn(normed, head_w[...])
    log_total = jnp.log(jnp.sum(jnp.exp(logits), axis=1, keepdims=True))
    is_target = column(targets[...]) == lax.broadcasted_iota(jnp.int32, logits.shape, 1)
    chosen = jnp.sum(jnp.where(is_target, logits, 0.0), axis=1, keepdims=True)
    log_probs[...] = jnp.transpose(jnp.broadcast_to(chosen - log_total, (N, N)))[:1, :]
    probs = jnp.exp(logits - log_total)
    logit_grads = (column(cotangent[...]) * (is_target.astype(F32) - probs)).astype(BF)
    scaled = nt(logit_grads, head_w[...]) * gains
    decoder_grads = inverse * (
        scaled - normal_part * jnp.mean(scaled * normal_part, axis=1, keepdims=True)
    )
    high = decoder_grads.astype(BF)
    low = (decoder_grads - high.astype(F32)).astype(BF)
    grads[z, x] = (nn(member_bf, high) + nn(member_bf, low)).astype(BF)

    grads_g = gather(grads, cut_cols, True)
    next(grads_g)
    state_grads[...] = decoder_grads
    run(grads_g)

    def backward(i, carry):
        rows = grads[i].reshape(ROWS, E)
        hidden_grads = nt(rows[:, :EH], fold_d[0].reshape(FB, EH)) + nt(rows[:, EH:], fold_d[1].reshape(FB, EH))
        g_gate[i] = (hidden_grads * gate_c[i]).astype(BF)
        g_up[i] = (hidden_grads * up_c[i]).astype(BF)
        g_mix[i] = nt(rows, w_out[...]).astype(BF)
        return carry

    lax.fori_loop(0, SIDE, backward, 0)

    def fill_grads(i, h):
        term = (
            nt(g_gate[i], fold_g[h].reshape(EH, FB))
            + nt(g_up[i], fold_u[h].reshape(EH, FB))
            + nt(g_mix[i], w_in[h * EH:(h + 1) * EH, :])
        )
        qout[i, :, :, h * EH:(h + 1) * EH] = term.astype(BF).reshape(SIDE, SLOTS, EH)

    pooled_grads = scatter_sum(1, fill_grads, qout)
    divisor_row = jnp.maximum(jnp.sum(member_t.astype(F32), axis=0, keepdims=True), 1.0)
    byte_divisor = jnp.sum(jnp.where(member_t, divisor_row, 0.0), axis=1, keepdims=True)
    state_grads[...] += nn(member_t_bf, pooled_grads) / byte_divisor

    @pl.when(z == y)
    def _():
        for copy in spread_in + spread_out:
            copy.wait_send()

    for copy in sends:
        copy.wait_send()


def body(
    states, patch_of, targets, cotangent, w_in, w_gate, w_up, w_down, w_out, head_gain, w_head
):
    n, E = states.shape
    DT = w_in.shape[1]
    DG, FB = w_gate.shape
    V = w_head.shape[1]
    EH = E // 2
    ER, FR, OR = EH // SIDE, FB // SIDE, DT // SIDE
    ROWS = SIDE * SLOTS
    vmem = lambda *shape: pltpu.VMEM(shape, BF)
    vmem32 = lambda *shape: pltpu.VMEM(shape, F32)
    scratch = [
        vmem(2, FB, DG), vmem(2, FB, DG), vmem(2, FB, DG), vmem(E, V),
        vmem(SIDE, SIDE, ER, DT), vmem(SIDE, SIDE, OR, EH),
        vmem(SIDE, SIDE, SLOTS, E),
        vmem(2, SIDE, ER, FB), vmem(2, SIDE, ER, FB), vmem(2, SIDE, FR, EH),
        vmem(SIDE, ER, FB), vmem(SIDE, ER, FB), vmem(SIDE, FR, EH),
        vmem(2, ER, FB), vmem(2, ER, FB), vmem(2, FR, EH),
        vmem(2, ER, FB), vmem(2, ER, FB), vmem(2, FR, EH),
        vmem(SIDE, ROWS, DT),
        vmem32(SIDE, ROWS, FB), vmem32(SIDE, ROWS, FB),
        vmem(SIDE, ROWS, FB),
        vmem(SIDE, SIDE, SLOTS, E), vmem(SIDE, SIDE, SLOTS, E),
        vmem(SIDE, ROWS, FB), vmem(SIDE, ROWS, FB), vmem(SIDE, ROWS, DT),
        vmem(SIDE, SIDE, SLOTS, E),
        vmem(2, 2, SIDE - 1, SIDE, SLOTS, EH), vmem(2, 2, SIDE - 1, SLOTS, EH),
        vmem(2, 2, SIDE, SLOTS, EH),
        pltpu.SemaphoreType.DMA((N_SEMS,)), pltpu.SemaphoreType.DMA((N_SEMS,)),
        pltpu.SemaphoreType.DMA((4,)),
    ]
    near = pl.BlockSpec(memory_space=pltpu.VMEM)
    away = pl.BlockSpec(memory_space=pl.ANY)
    log_probs, state_grads = pl.pallas_call(
        kernel,
        out_shape=(jax.ShapeDtypeStruct((1, n), F32), jax.ShapeDtypeStruct((n, E), F32)),
        in_specs=[near] * 5 + [away] * 3 + [near] * 2 + [away],
        out_specs=(near, near),
        scratch_shapes=scratch,
        compiler_params=pltpu.CompilerParams(
            collective_id=0, has_side_effects=True, vmem_limit_bytes=60 * 2**20
        ),
        name="patch_step",
    )(
        states, patch_of.reshape(1, n), targets.reshape(1, n), cotangent.reshape(1, n),
        w_in, w_gate.T, w_up.T, w_down, w_out, head_gain, w_head,
    )
    return log_probs.reshape(n), state_grads


def solution(mesh):
    return jax.shard_map(
        body,
        mesh=mesh,
        in_specs=(
            P(("grp", "tp"), None),
            P(("grp", "tp")),
            P(("grp", "tp")),
            P(("grp", "tp")),
            P(None, "tp"),
            P("grp", "tp"),
            P("grp", "tp"),
            P("tp", "grp"),
            P("tp", None),
            P(),
            P(),
        ),
        out_specs=(P(("grp", "tp")), P(("grp", "tp"), None)),
        check_vma=False,
    )
```

```python
import jax
import jax.numpy as jnp
from jax import lax
from jax.experimental import pallas as pl
from jax.experimental.pallas import tpu as pltpu
from jax.sharding import PartitionSpec as P

BF = jnp.bfloat16
F32 = jnp.float32
MESH = pl.DeviceIdType.MESH
SIDE = 4
SLOTS = 48
N_SEMS = 256


def nn(a, b):
    return lax.dot_general(a, b, (((1,), (0,)), ((), ())), preferred_element_type=F32)


def nt(a, b):
    return lax.dot_general(a, b, (((1,), (1,)), ((), ())), preferred_element_type=F32)


def wrap(v):
    return lax.rem(v, SIDE)


def kernel(
    states, patch_of, targets, cotangent, w_in, w_gate, w_up, w_down, w_out, gain, w_head,
    log_probs, state_grads,
    raw_g, raw_u, raw_d, head_w, slab_in, slab_out, pool, fold_g, fold_u, fold_d,
    part_g, part_u, part_d, edge_g, edge_u, edge_d, mid_g, mid_u, mid_d,
    act, gate_c, up_c, hid, pout, qout, g_gate, g_up, g_mix, grads,
    rs1, rs2, mid1,
    ssem, rsem, lsem,
):
    N, E = states.shape
    EH = E // 2
    FB = w_gate.shape[0]
    DT = w_in.shape[1]
    ER = EH // SIDE
    FR = FB // SIDE
    OR = DT // SIDE
    ROWS = SIDE * SLOTS

    g = lax.axis_index("grp")
    t = lax.axis_index("tp")
    y, c = g // 2, g % 2
    z, x = t // SIDE, t % SIDE

    def X(d):
        return (g, SIDE * z + wrap(x + d))

    def Z(d):
        return (g, SIDE * wrap(z + d) + x)

    def Y(d):
        return (2 * wrap(y + d) + c, t)

    partner = (2 * y + (1 - c), t)

    sends = []
    count = [0]

    def new_sem():
        count[0] += 1
        return count[0] - 1

    def remote(src, dst, device):
        i = new_sem()
        copy = pltpu.make_async_remote_copy(
            src_ref=src, dst_ref=dst, send_sem=ssem.at[i], recv_sem=rsem.at[i],
            device_id=device, device_id_type=MESH,
        )
        copy.start()
        sends.append(copy)
        return copy

    def arrive(copies):
        for copy in copies:
            copy.wait_recv()

    barrier = pltpu.get_barrier_semaphore()
    peers = [X(d) for d in (1, 2, 3)] + [Z(d) for d in (1, 2, 3)] + [Y(1), Y(3), partner]
    for peer in peers:
        pl.semaphore_signal(barrier, 1, device_id=peer, device_id_type=MESH)

    local = [
        pltpu.make_async_copy(src, dst, lsem.at[i])
        for i, (src, dst) in enumerate(
            ((w_gate, raw_g.at[c]), (w_up, raw_u.at[c]), (w_down, raw_d.at[c]), (w_head, head_w))
        )
    ]
    for copy in local:
        copy.start()

    def column(row):
        return jnp.transpose(jnp.broadcast_to(row, (N, N)))[:, :1]

    member = patch_of[...] == lax.broadcasted_iota(jnp.int32, (SLOTS, N), 0)
    member_bf = member.astype(BF)
    divisor = jnp.maximum(jnp.sum(member.astype(F32), axis=1, keepdims=True), 1.0)
    pool[z, x] = (nn(member_bf, states[...]) / divisor).astype(BF)

    pl.semaphore_wait(barrier, len(peers))

    def spread(src_of, dst_of):
        first = [new_sem() for _ in range(SIDE)]
        out = []
        for d in range(1, SIDE):
            zz = wrap(z + d)
            out.append(
                pltpu.make_async_remote_copy(
                    src_ref=src_of(zz), dst_ref=dst_of(zz), send_sem=ssem.at[first[d]],
                    recv_sem=rsem.at[first[0]], device_id=Z(d), device_id_type=MESH,
                )
            )
        return out

    spread_in = spread(
        lambda zz: w_in.at[pl.ds(pl.multiple_of(c * EH + zz * ER, 16), ER), :],
        lambda zz: slab_in.at[zz, x],
    )

    spread_out = spread(
        lambda zz: w_out.at[
            pl.ds(pl.multiple_of(zz * OR, 16), OR), pl.ds(pl.multiple_of(c * EH, 128), EH)
        ],
        lambda zz: slab_out.at[zz, x],
    )

    def spread_start(copies):
        @pl.when(z == y)
        def _():
            for copy in copies:
                copy.start()

    def spread_arrive(copies):
        @pl.when(z != y)
        def _():
            copies[0].wait_recv()

    spread_start(spread_in)
    spread_start(spread_out)

    swap = []
    for src, dst in ((w_gate, raw_g), (w_up, raw_u), (w_down, raw_d)):
        swap.append(remote(src, dst.at[c], partner))

    @pl.when(z == y)
    def _():
        slab_in[z, x] = w_in[pl.ds(pl.multiple_of(c * EH + z * ER, 16), ER), :]
        piece = w_out[pl.ds(pl.multiple_of(z * OR, 16), OR), :]
        slab_out[z, x] = jnp.where(c == 0, piece[:, :EH], piece[:, EH:])

    def gather(buf, cut, ring):
        def slot(h, f, s, piece=None):
            at = (wrap(z + s + 4), wrap(x + f + 4)) if h == 0 else (wrap(z + f + 4), wrap(x + s + 4))
            return buf.at[at + cut(h, piece)]

        def first(h, d):
            return X(d) if h == 0 else Z(d)

        def second(h, d):
            return Z(d) if h == 0 else X(d)

        def send(ref, device):
            return remote(ref, ref, device)

        ways = (1, 3) if ring else (1, 3, 2)
        one, two, last = {}, {}, []
        for d in (1, 3, 2):
            for h in range(2):
                one[h, d] = send(slot(h, 0, 0), first(h, d))
        for e in ways:
            for h in range(2):
                two[h, 0, e] = send(slot(h, 0, 0), second(h, e))
        yield
        for d in (1, 3, 2):
            for h in range(2):
                one[h, d].wait_recv()
                for e in ways:
                    two[h, d, e] = send(slot(h, -d, 0), second(h, e))
        yield
        if ring:
            for d in (0, 1, 3, 2):
                for e in ways:
                    for h in range(2):
                        two[h, d, e].wait_recv()
                        last.append(send(slot(h, -d, -e, e // 2), second(h, e)))
                yield
            arrive(last)
        else:
            arrive(two.values())

    def cut_rows(rows, split):
        def cut(h, piece):
            lo, hi = h * rows // 2, (h + 1) * rows // 2
            mid = lo + split[h]
            if piece == 0:
                hi = mid
            elif piece == 1:
                lo = mid
            return (slice(lo, hi), slice(None))
        return cut

    def cut_cols(h, piece):
        lo, hi = h * EH, (h + 1) * EH
        mid = lo + (384 if h == 0 else 256)
        if piece == 0:
            hi = mid
        elif piece == 1:
            lo = mid
        return (slice(None), slice(lo, hi))

    def run(gen):
        for _ in gen:
            pass

    in_g = gather(slab_in, cut_rows(ER, (48, 32)), False)
    out_g = gather(slab_out, cut_rows(OR, (16, 16)), False)
    pool_g = gather(pool, cut_cols, False)

    spread_arrive(spread_in)
    next(in_g)
    next(in_g)
    spread_arrive(spread_out)
    next(out_g)
    run(in_g)
    arrive(swap[:2])
    for copy in local[:2]:
        copy.wait()

    def block_in(raw):
        def f():
            total = jnp.zeros((EH, FB), F32)
            for xx in range(SIDE):
                lo = (xx % 2) * DT
                total += nt(slab_in[:, xx].reshape(EH, DT), raw[xx // 2, :, lo:lo + DT])
            return total.astype(BF).reshape(SIDE, ER, FB)
        return f

    def block_down():
        total = jnp.zeros((FB, EH), F32)
        for xx in range(SIDE):
            lo = (xx % 2) * DT
            total += nn(raw_d[xx // 2, :, lo:lo + DT], slab_out[:, xx].reshape(DT, EH))
        return total.astype(BF).reshape(SIDE, FR, EH)

    class Fold:
        def __init__(self, block, part, edge, mid, out, split):
            self.block, self.part, self.edge, self.mid, self.split = block, part, edge, mid, split
            self.out = out

        def step_1(self):
            if self.block is not None:
                self.part[...] = self.block()
            s = self.split
            far = wrap(y + 2)
            self.one = [
                remote(self.part.at[far, :s], self.edge.at[0, :s], Y(1)),
                remote(self.part.at[far, s:], self.edge.at[1, s:], Y(3)),
            ]

        def step_2(self):
            s = self.split
            right, left = wrap(y + 1), wrap(y + 3)
            self.one[0].wait_recv()
            self.part[right, :s] = (self.part[right, :s].astype(F32) + self.edge[0, :s].astype(F32)).astype(BF)
            two = [remote(self.part.at[right], self.mid.at[0], Y(1))]
            self.one[1].wait_recv()
            self.part[left, s:] = (self.part[left, s:].astype(F32) + self.edge[1, s:].astype(F32)).astype(BF)
            self.two = two + [remote(self.part.at[left], self.mid.at[1], Y(3))]

        def step_3(self):
            arrive(self.two)
            total = self.part[y].astype(F32) + self.mid[0].astype(F32) + self.mid[1].astype(F32)
            own = self.out(y)
            own[...] = total.astype(BF)
            self.three = [remote(own, own, Y(1)), remote(own, own, Y(3))]
            self.cross = [remote(own, own, partner)]

        def step_4(self):
            s = self.split
            self.three[0].wait_recv()
            low = self.out(wrap(y + 3))
            four = [remote(low.at[:s], low.at[:s], Y(1))]
            self.cross.append(remote(low, low, partner))
            self.three[1].wait_recv()
            high = self.out(wrap(y + 1))
            four.append(remote(high.at[s:], high.at[s:], Y(3)))
            self.cross.append(remote(high, high, partner))
            self.four = four

        def step_5(self):
            arrive(self.four)
            far = self.out(wrap(y + 2))
            self.cross.append(remote(far, far, partner))
            arrive(self.cross)

    gate_f = Fold(block_in(raw_g), part_g, edge_g, mid_g, lambda yy: fold_g.at[c, yy], ER // 2)
    up_f = Fold(block_in(raw_u), part_u, edge_u, mid_u, lambda yy: fold_u.at[c, yy], ER // 2)

    def fold_down(rows, split):
        return Fold(
            None, part_d.at[:, rows], edge_d.at[:, rows], mid_d.at[:, rows],
            lambda yy: fold_d.at[c, yy, rows], split,
        )

    downs = [fold_down(slice(0, 64), 32), fold_down(slice(64, FR), 32)]

    def down_step(name):
        for fold in downs:
            getattr(fold, name)()

    gate_f.step_1()
    up_f.step_1()
    next(out_g)
    next(pool_g)
    gate_f.step_2()
    up_f.step_2()
    run(out_g)
    arrive(swap[2:])
    local[2].wait()
    part_d[...] = block_down()
    down_step("step_1")
    next(pool_g)
    gate_f.step_3()
    up_f.step_3()
    down_step("step_2")
    gate_f.step_4()
    up_f.step_4()
    down_step("step_3")
    gate_f.step_5()
    up_f.step_5()
    run(pool_g)

    def forward(i, carry):
        rows = pool[i].reshape(ROWS, E)
        act[i] = nn(rows, w_in[...]).astype(BF)
        gate_pre = nn(rows, fold_g[...].reshape(E, FB))
        up_pre = nn(rows, fold_u[...].reshape(E, FB))
        s = 1.0 / (1.0 + jnp.exp(-gate_pre))
        silu = gate_pre * s
        hid[i] = (silu * up_pre).astype(BF)
        gate_c[i] = up_pre * s * (1.0 + gate_pre * (1.0 - s))
        up_c[i] = silu
        return carry

    lax.fori_loop(0, 1, forward, 0)
    down_step("step_4")
    lax.fori_loop(1, SIDE, forward, 0)
    down_step("step_5")

    def scatter_sum(k, fill, buf):
        one, two = {}, {}

        def cols(h):
            return slice(h * EH, (h + 1) * EH)

        def send_one(h, p, q):
            at = (wrap(z + p), wrap(x + q)) if h == 0 else (wrap(z + q), wrap(x + p))
            one[h, q, p] = remote(
                buf.at[at + (slice(None), cols(h))], rs1.at[k, h, p - 1, q], Z(p) if h == 0 else X(p)
            )

        def send_all(h, q):
            for p in (1, 3, 2):
                send_one(h, p, q)

        fill(wrap(z + 2), 0)
        send_one(0, 2, 2)
        fill(wrap(z + 2), 1)
        send_all(1, 2)
        for d in (1, 3):
            fill(wrap(z + d), 0)
            send_one(0, d, 2)
        send_all(0, 1)
        fill(wrap(z + 1), 1)
        send_all(1, 1)
        send_all(0, 3)
        fill(wrap(z + 3), 1)
        send_all(1, 3)
        send_all(0, 0)
        fill(z, 1)
        send_all(1, 0)
        fill(z, 0)
        halves = {}
        for q in (2, 1, 3, 0):
            for h in (1, 0):
                at = (z, wrap(x + q)) if h == 0 else (wrap(z + q), x)
                for p in (1, 3, 2):
                    one[h, q, p].wait_recv()
                total = buf[at + (slice(None), cols(h))].astype(F32)
                for p in range(SIDE - 1):
                    total += rs1[k, h, p, q].astype(F32)
                if q:
                    mid1[k, h, q] = total.astype(BF)
                    two[h, q] = remote(
                        mid1.at[k, h, q], rs2.at[k, h, q - 1], X(q) if h == 0 else Z(q)
                    )
                else:
                    halves[h] = total
        for h in range(2):
            total = halves[h]
            for q in (1, 3, 2):
                two[h, q].wait_recv()
                total += rs2[k, h, q - 1].astype(F32)
            halves[h] = total.astype(BF)
        return jnp.concatenate([halves[0], halves[1]], axis=1)

    def fill_out(i, h):
        term = nn(hid[i], fold_d[h].reshape(FB, EH)) + nn(act[i], w_out[:, h * EH:(h + 1) * EH])
        pout[i, :, :, h * EH:(h + 1) * EH] = term.astype(BF).reshape(SIDE, SLOTS, EH)

    patch_out = scatter_sum(0, fill_out, pout)

    patch_col = column(patch_of[...])
    member_t = patch_col == lax.broadcasted_iota(jnp.int32, (N, SLOTS), 1)
    member_t_bf = member_t.astype(BF)
    decoder_in = states[...].astype(F32) + nn(member_t_bf, patch_out)
    inverse = lax.rsqrt(jnp.mean(decoder_in * decoder_in, axis=1, keepdims=True) + 1e-06)
    normal_part = decoder_in * inverse
    gains = gain[...].reshape(1, E)
    normed = (normal_part * gains).astype(BF)
    local[3].wait()
    logits = nn(normed, head_w[...])
    log_total = jnp.log(jnp.sum(jnp.exp(logits), axis=1, keepdims=True))
    is_target = column(targets[...]) == lax.broadcasted_iota(jnp.int32, logits.shape, 1)
    chosen = jnp.sum(jnp.where(is_target, logits, 0.0), axis=1, keepdims=True)
    log_probs[...] = jnp.transpose(jnp.broadcast_to(chosen - log_total, (N, N)))[:1, :]
    probs = jnp.exp(logits - log_total)
    logit_grads = (column(cotangent[...]) * (is_target.astype(F32) - probs)).astype(BF)
    scaled = nt(logit_grads, head_w[...]) * gains
    decoder_grads = inverse * (
        scaled - normal_part * jnp.mean(scaled * normal_part, axis=1, keepdims=True)
    )
    high = decoder_grads.astype(BF)
    low = (decoder_grads - high.astype(F32)).astype(BF)
    grads[z, x] = (nn(member_bf, high) + nn(member_bf, low)).astype(BF)

    grads_g = gather(grads, cut_cols, True)
    next(grads_g)
    state_grads[...] = decoder_grads
    run(grads_g)

    def backward(i, carry):
        rows = grads[i].reshape(ROWS, E)
        hidden_grads = nt(rows[:, :EH], fold_d[0].reshape(FB, EH)) + nt(rows[:, EH:], fold_d[1].reshape(FB, EH))
        g_gate[i] = (hidden_grads * gate_c[i]).astype(BF)
        g_up[i] = (hidden_grads * up_c[i]).astype(BF)
        g_mix[i] = nt(rows, w_out[...]).astype(BF)
        return carry

    lax.fori_loop(0, SIDE, backward, 0)

    def fill_grads(i, h):
        term = (
            nt(g_gate[i], fold_g[h].reshape(EH, FB))
            + nt(g_up[i], fold_u[h].reshape(EH, FB))
            + nt(g_mix[i], w_in[h * EH:(h + 1) * EH, :])
        )
        qout[i, :, :, h * EH:(h + 1) * EH] = term.astype(BF).reshape(SIDE, SLOTS, EH)

    pooled_grads = scatter_sum(1, fill_grads, qout)
    divisor_row = jnp.maximum(jnp.sum(member_t.astype(F32), axis=0, keepdims=True), 1.0)
    byte_divisor = jnp.sum(jnp.where(member_t, divisor_row, 0.0), axis=1, keepdims=True)
    state_grads[...] += nn(member_t_bf, pooled_grads) / byte_divisor

    @pl.when(z == y)
    def _():
        for copy in spread_in + spread_out:
            copy.wait_send()

    for copy in sends:
        copy.wait_send()
    assert count[0] <= N_SEMS


def body(
    states, patch_of, targets, cotangent, w_in, w_gate, w_up, w_down, w_out, head_gain, w_head
):
    n, E = states.shape
    DT = w_in.shape[1]
    DG, FB = w_gate.shape
    V = w_head.shape[1]
    EH = E // 2
    ER, FR, OR = EH // SIDE, FB // SIDE, DT // SIDE
    ROWS = SIDE * SLOTS
    vmem = lambda *shape: pltpu.VMEM(shape, BF)
    vmem32 = lambda *shape: pltpu.VMEM(shape, F32)
    scratch = [
        vmem(2, FB, DG), vmem(2, FB, DG), vmem(2, FB, DG), vmem(E, V),
        vmem(SIDE, SIDE, ER, DT), vmem(SIDE, SIDE, OR, EH),
        vmem(SIDE, SIDE, SLOTS, E),
        vmem(2, SIDE, ER, FB), vmem(2, SIDE, ER, FB), vmem(2, SIDE, FR, EH),
        vmem(SIDE, ER, FB), vmem(SIDE, ER, FB), vmem(SIDE, FR, EH),
        vmem(2, ER, FB), vmem(2, ER, FB), vmem(2, FR, EH),
        vmem(2, ER, FB), vmem(2, ER, FB), vmem(2, FR, EH),
        vmem(SIDE, ROWS, DT),
        vmem32(SIDE, ROWS, FB), vmem32(SIDE, ROWS, FB),
        vmem(SIDE, ROWS, FB),
        vmem(SIDE, SIDE, SLOTS, E), vmem(SIDE, SIDE, SLOTS, E),
        vmem(SIDE, ROWS, FB), vmem(SIDE, ROWS, FB), vmem(SIDE, ROWS, DT),
        vmem(SIDE, SIDE, SLOTS, E),
        vmem(2, 2, SIDE - 1, SIDE, SLOTS, EH), vmem(2, 2, SIDE - 1, SLOTS, EH),
        vmem(2, 2, SIDE, SLOTS, EH),
        pltpu.SemaphoreType.DMA((N_SEMS,)), pltpu.SemaphoreType.DMA((N_SEMS,)),
        pltpu.SemaphoreType.DMA((4,)),
    ]
    near = pl.BlockSpec(memory_space=pltpu.VMEM)
    away = pl.BlockSpec(memory_space=pl.ANY)
    log_probs, state_grads = pl.pallas_call(
        kernel,
        out_shape=(jax.ShapeDtypeStruct((1, n), F32), jax.ShapeDtypeStruct((n, E), F32)),
        in_specs=[near] * 5 + [away] * 3 + [near] * 2 + [away],
        out_specs=(near, near),
        scratch_shapes=scratch,
        compiler_params=pltpu.CompilerParams(
            collective_id=0, has_side_effects=True, vmem_limit_bytes=60 * 2**20
        ),
        name="patch_step",
    )(
        states, patch_of.reshape(1, n), targets.reshape(1, n), cotangent.reshape(1, n),
        w_in, w_gate.T, w_up.T, w_down, w_out, head_gain, w_head,
    )
    return log_probs.reshape(n), state_grads


def solution(mesh):
    return jax.shard_map(
        body,
        mesh=mesh,
        in_specs=(
            P(("grp", "tp"), None),
            P(("grp", "tp")),
            P(("grp", "tp")),
            P(("grp", "tp")),
            P(None, "tp"),
            P("grp", "tp"),
            P("grp", "tp"),
            P("tp", "grp"),
            P("tp", None),
            P(),
            P(),
        ),
        out_specs=(P(("grp", "tp")), P(("grp", "tp"), None)),
        check_vma=False,
    )
```

```python
import jax
import jax.numpy as jnp
from jax import lax
from jax.experimental import pallas as pl
from jax.experimental.pallas import tpu as pltpu
from jax.sharding import PartitionSpec as P

BF = jnp.bfloat16
F32 = jnp.float32
MESH = pl.DeviceIdType.MESH
SIDE = 4
SLOTS = 48
N_SEMS = 256


def nn(a, b):
    return lax.dot_general(a, b, (((1,), (0,)), ((), ())), preferred_element_type=F32)


def nt(a, b):
    return lax.dot_general(a, b, (((1,), (1,)), ((), ())), preferred_element_type=F32)


def wrap(v):
    return lax.rem(v, SIDE)


def kernel(
    states, patch_of, targets, cotangent, w_in, w_gate, w_up, w_down, w_out, gain, w_head,
    log_probs, state_grads, spread_grads,
    raw_g, raw_u, raw_d, head_w, slab_in, slab_out, pool, fold_g, fold_u, fold_d,
    part_g, part_u, part_d, edge_g, edge_u, edge_d, mid_g, mid_u, mid_d,
    act, gate_c, up_c, hid, pout, qout, g_gate, g_up, g_mix, grads,
    rs1, rs2, mid1,
    ssem, rsem, lsem,
):
    N, E = states.shape
    EH = E // 2
    FB = w_gate.shape[0]
    DT = w_in.shape[1]
    ER = EH // SIDE
    FR = FB // SIDE
    OR = DT // SIDE
    ROWS = SIDE * SLOTS

    g = lax.axis_index("grp")
    t = lax.axis_index("tp")
    y, c = g // 2, g % 2
    z, x = t // SIDE, t % SIDE

    def X(d):
        return (g, SIDE * z + wrap(x + d))

    def Z(d):
        return (g, SIDE * wrap(z + d) + x)

    def Y(d):
        return (2 * wrap(y + d) + c, t)

    partner = (2 * y + (1 - c), t)

    sends = []
    count = [0]

    def new_sem():
        count[0] += 1
        return count[0] - 1

    def remote(src, dst, device):
        i = new_sem()
        copy = pltpu.make_async_remote_copy(
            src_ref=src, dst_ref=dst, send_sem=ssem.at[i], recv_sem=rsem.at[i],
            device_id=device, device_id_type=MESH,
        )
        copy.start()
        sends.append(copy)
        return copy

    def arrive(copies):
        for copy in copies:
            copy.wait_recv()

    barrier = pltpu.get_barrier_semaphore()
    peers = [X(d) for d in (1, 2, 3)] + [Z(d) for d in (1, 2, 3)] + [Y(1), Y(3), partner]
    for peer in peers:
        pl.semaphore_signal(barrier, 1, device_id=peer, device_id_type=MESH)

    local = [
        pltpu.make_async_copy(src, dst, lsem.at[i])
        for i, (src, dst) in enumerate(
            ((w_gate, raw_g.at[c]), (w_up, raw_u.at[c]), (w_down, raw_d.at[c]), (w_head, head_w))
        )
    ]
    for copy in local:
        copy.start()

    def column(row):
        return jnp.transpose(jnp.broadcast_to(row, (N, N)))[:, :1]

    member = patch_of[...] == lax.broadcasted_iota(jnp.int32, (SLOTS, N), 0)
    member_bf = member.astype(BF)
    divisor = jnp.maximum(jnp.sum(member.astype(F32), axis=1, keepdims=True), 1.0)
    pool[z, x] = (nn(member_bf, states[...]) / divisor).astype(BF)

    pl.semaphore_wait(barrier, len(peers))

    def spread(src_of, dst_of):
        first = [new_sem() for _ in range(SIDE)]
        out = []
        for d in range(1, SIDE):
            zz = wrap(z + d)
            out.append(
                pltpu.make_async_remote_copy(
                    src_ref=src_of(zz), dst_ref=dst_of(zz), send_sem=ssem.at[first[d]],
                    recv_sem=rsem.at[first[0]], device_id=Z(d), device_id_type=MESH,
                )
            )
        return out

    spread_in = spread(
        lambda zz: w_in.at[pl.ds(pl.multiple_of(c * EH + zz * ER, 16), ER), :],
        lambda zz: slab_in.at[zz, x],
    )

    spread_out = spread(
        lambda zz: w_out.at[
            pl.ds(pl.multiple_of(zz * OR, 16), OR), pl.ds(pl.multiple_of(c * EH, 128), EH)
        ],
        lambda zz: slab_out.at[zz, x],
    )

    def spread_start(copies):
        @pl.when(z == y)
        def _():
            for copy in copies:
                copy.start()

    def spread_arrive(copies):
        @pl.when(z != y)
        def _():
            copies[0].wait_recv()

    spread_start(spread_in)
    spread_start(spread_out)

    swap = []
    for src, dst in ((w_gate, raw_g), (w_up, raw_u), (w_down, raw_d)):
        swap.append(remote(src, dst.at[c], partner))

    @pl.when(z == y)
    def _():
        slab_in[z, x] = w_in[pl.ds(pl.multiple_of(c * EH + z * ER, 16), ER), :]
        piece = w_out[pl.ds(pl.multiple_of(z * OR, 16), OR), :]
        slab_out[z, x] = jnp.where(c == 0, piece[:, :EH], piece[:, EH:])

    def gather(buf, cut, ring):
        def slot(h, f, s, piece=None):
            at = (wrap(z + s + 4), wrap(x + f + 4)) if h == 0 else (wrap(z + f + 4), wrap(x + s + 4))
            return buf.at[at + cut(h, piece)]

        def first(h, d):
            return X(d) if h == 0 else Z(d)

        def second(h, d):
            return Z(d) if h == 0 else X(d)

        def send(ref, device):
            return remote(ref, ref, device)

        ways = (1, 3) if ring else (1, 3, 2)
        one, two, last = {}, {}, []
        for d in (1, 3, 2):
            for h in range(2):
                one[h, d] = send(slot(h, 0, 0), first(h, d))
        for e in ways:
            for h in range(2):
                two[h, 0, e] = send(slot(h, 0, 0), second(h, e))
        yield
        for d in (1, 3, 2):
            for h in range(2):
                one[h, d].wait_recv()
                for e in ways:
                    two[h, d, e] = send(slot(h, -d, 0), second(h, e))
        yield
        if ring:
            for d in (0, 1, 3, 2):
                for e in ways:
                    for h in range(2):
                        two[h, d, e].wait_recv()
                        last.append(send(slot(h, -d, -e, e // 2), second(h, e)))
                yield
            arrive(last)
        else:
            arrive(two.values())

    def cut_rows(rows, split):
        def cut(h, piece):
            lo, hi = h * rows // 2, (h + 1) * rows // 2
            mid = lo + split[h]
            if piece == 0:
                hi = mid
            elif piece == 1:
                lo = mid
            return (slice(lo, hi), slice(None))
        return cut

    def cut_cols(h, piece):
        lo, hi = h * EH, (h + 1) * EH
        mid = lo + (384 if h == 0 else 256)
        if piece == 0:
            hi = mid
        elif piece == 1:
            lo = mid
        return (slice(None), slice(lo, hi))

    def run(gen):
        for _ in gen:
            pass

    in_g = gather(slab_in, cut_rows(ER, (48, 32)), False)
    out_g = gather(slab_out, cut_rows(OR, (16, 16)), False)
    pool_g = gather(pool, cut_cols, False)

    spread_arrive(spread_in)
    next(in_g)
    next(in_g)
    spread_arrive(spread_out)
    next(out_g)
    run(in_g)
    arrive(swap[:2])
    for copy in local[:2]:
        copy.wait()

    def block_in(raw):
        def f():
            total = jnp.zeros((EH, FB), F32)
            for xx in range(SIDE):
                lo = (xx % 2) * DT
                total += nt(slab_in[:, xx].reshape(EH, DT), raw[xx // 2, :, lo:lo + DT])
            return total.astype(BF).reshape(SIDE, ER, FB)
        return f

    def block_down():
        total = jnp.zeros((FB, EH), F32)
        for xx in range(SIDE):
            lo = (xx % 2) * DT
            total += nn(raw_d[xx // 2, :, lo:lo + DT], slab_out[:, xx].reshape(DT, EH))
        return total.astype(BF).reshape(SIDE, FR, EH)

    class Fold:
        def __init__(self, block, part, edge, mid, out, split):
            self.block, self.part, self.edge, self.mid, self.split = block, part, edge, mid, split
            self.out = out

        def step_1(self):
            if self.block is not None:
                self.part[...] = self.block()
            s = self.split
            far = wrap(y + 2)
            self.one = [
                remote(self.part.at[far, :s], self.edge.at[0, :s], Y(1)),
                remote(self.part.at[far, s:], self.edge.at[1, s:], Y(3)),
            ]

        def step_2(self):
            s = self.split
            right, left = wrap(y + 1), wrap(y + 3)
            self.one[0].wait_recv()
            self.part[right, :s] = (self.part[right, :s].astype(F32) + self.edge[0, :s].astype(F32)).astype(BF)
            two = [remote(self.part.at[right], self.mid.at[0], Y(1))]
            self.one[1].wait_recv()
            self.part[left, s:] = (self.part[left, s:].astype(F32) + self.edge[1, s:].astype(F32)).astype(BF)
            self.two = two + [remote(self.part.at[left], self.mid.at[1], Y(3))]

        def step_3(self):
            arrive(self.two)
            total = self.part[y].astype(F32) + self.mid[0].astype(F32) + self.mid[1].astype(F32)
            own = self.out(y)
            own[...] = total.astype(BF)
            self.three = [remote(own, own, Y(1)), remote(own, own, Y(3))]
            self.cross = [remote(own, own, partner)]

        def step_4(self):
            s = self.split
            self.three[0].wait_recv()
            low = self.out(wrap(y + 3))
            four = [remote(low.at[:s], low.at[:s], Y(1))]
            self.cross.append(remote(low, low, partner))
            self.three[1].wait_recv()
            high = self.out(wrap(y + 1))
            four.append(remote(high.at[s:], high.at[s:], Y(3)))
            self.cross.append(remote(high, high, partner))
            self.four = four

        def step_5(self):
            arrive(self.four)
            far = self.out(wrap(y + 2))
            self.cross.append(remote(far, far, partner))
            arrive(self.cross)

    gate_f = Fold(block_in(raw_g), part_g, edge_g, mid_g, lambda yy: fold_g.at[c, yy], ER // 2)
    up_f = Fold(block_in(raw_u), part_u, edge_u, mid_u, lambda yy: fold_u.at[c, yy], ER // 2)

    def fold_down(rows, split):
        return Fold(
            None, part_d.at[:, rows], edge_d.at[:, rows], mid_d.at[:, rows],
            lambda yy: fold_d.at[c, yy, rows], split,
        )

    downs = [fold_down(slice(0, 64), 32), fold_down(slice(64, FR), 32)]

    def down_step(name):
        for fold in downs:
            getattr(fold, name)()

    gate_f.step_1()
    up_f.step_1()
    next(out_g)
    next(pool_g)
    gate_f.step_2()
    up_f.step_2()

    patch_col = column(patch_of[...])
    member_t = patch_col == lax.broadcasted_iota(jnp.int32, (N, SLOTS), 1)
    member_t_bf = member_t.astype(BF)
    divisor_row = jnp.maximum(jnp.sum(member_t.astype(F32), axis=0, keepdims=True), 1.0)
    byte_divisor = jnp.sum(jnp.where(member_t, divisor_row, 0.0), axis=1, keepdims=True)
    target_col = column(targets[...])
    weight_col = column(cotangent[...])

    run(out_g)
    arrive(swap[2:])
    local[2].wait()
    part_d[...] = block_down()
    down_step("step_1")
    next(pool_g)
    gate_f.step_3()
    up_f.step_3()
    down_step("step_2")
    gate_f.step_4()
    up_f.step_4()
    down_step("step_3")
    gate_f.step_5()
    up_f.step_5()
    run(pool_g)

    def forward(i, carry):
        rows = pool[i].reshape(ROWS, E)
        act[i] = nn(rows, w_in[...]).astype(BF)
        gate_pre = nn(rows, fold_g[...].reshape(E, FB))
        up_pre = nn(rows, fold_u[...].reshape(E, FB))
        s = 1.0 / (1.0 + jnp.exp(-gate_pre))
        silu = gate_pre * s
        hid[i] = (silu * up_pre).astype(BF)
        gate_c[i] = up_pre * s * (1.0 + gate_pre * (1.0 - s))
        up_c[i] = silu
        return carry

    down_step("step_4")
    lax.fori_loop(0, SIDE, forward, 0)
    down_step("step_5")

    def scatter_sum(k, prepare, fill, buf):
        one, two = {}, {}

        def cols(h):
            return slice(h * EH, (h + 1) * EH)

        def send_one(h, p, q):
            at = (wrap(z + p), wrap(x + q)) if h == 0 else (wrap(z + q), wrap(x + p))
            one[h, q, p] = remote(
                buf.at[at + (slice(None), cols(h))], rs1.at[k, h, p - 1, q], Z(p) if h == 0 else X(p)
            )

        def send_all(h, q):
            for p in (1, 3, 2):
                send_one(h, p, q)

        prepare(wrap(z + 2))
        fill(wrap(z + 2), 0)
        send_one(0, 2, 2)
        fill(wrap(z + 2), 1)
        send_all(1, 2)
        for d in (1, 3):
            prepare(wrap(z + d))
            fill(wrap(z + d), 0)
            send_one(0, d, 2)
        send_all(0, 1)
        fill(wrap(z + 1), 1)
        send_all(1, 1)
        send_all(0, 3)
        fill(wrap(z + 3), 1)
        send_all(1, 3)
        send_all(0, 0)
        prepare(z)
        fill(z, 1)
        send_all(1, 0)
        fill(z, 0)
        halves = {}
        for q in (2, 1, 3, 0):
            for h in (1, 0):
                at = (z, wrap(x + q)) if h == 0 else (wrap(z + q), x)
                for p in (1, 3, 2):
                    one[h, q, p].wait_recv()
                total = buf[at + (slice(None), cols(h))].astype(F32)
                for p in range(SIDE - 1):
                    total += rs1[k, h, p, q].astype(F32)
                if q:
                    mid1[k, h, q] = total.astype(BF)
                    two[h, q] = remote(
                        mid1.at[k, h, q], rs2.at[k, h, q - 1], X(q) if h == 0 else Z(q)
                    )
                else:
                    halves[h] = total
        for h in range(2):
            total = halves[h]
            for q in (1, 3, 2):
                two[h, q].wait_recv()
                total += rs2[k, h, q - 1].astype(F32)
            halves[h] = total.astype(BF)
        return jnp.concatenate([halves[0], halves[1]], axis=1)

    def fill_out(i, h):
        term = nn(hid[i], fold_d[h].reshape(FB, EH)) + nn(act[i], w_out[:, h * EH:(h + 1) * EH])
        pout[i, :, :, h * EH:(h + 1) * EH] = term.astype(BF).reshape(SIDE, SLOTS, EH)

    patch_out = scatter_sum(0, lambda i: None, fill_out, pout)

    decoder_in = states[...].astype(F32) + nn(member_t_bf, patch_out)
    inverse = lax.rsqrt(jnp.mean(decoder_in * decoder_in, axis=1, keepdims=True) + 1e-06)
    normal_part = decoder_in * inverse
    gains = gain[...].reshape(1, E)
    normed = (normal_part * gains).astype(BF)
    local[3].wait()
    logits = nn(normed, head_w[...])
    log_total = jnp.log(jnp.sum(jnp.exp(logits), axis=1, keepdims=True))
    is_target = target_col == lax.broadcasted_iota(jnp.int32, logits.shape, 1)
    chosen = jnp.sum(jnp.where(is_target, logits, 0.0), axis=1, keepdims=True)
    log_probs[...] = jnp.transpose(jnp.broadcast_to(chosen - log_total, (N, N)))[:1, :]
    probs = jnp.exp(logits - log_total)
    logit_grads = (weight_col * (is_target.astype(F32) - probs)).astype(BF)
    scaled = nt(logit_grads, head_w[...]) * gains
    decoder_grads = inverse * (
        scaled - normal_part * jnp.mean(scaled * normal_part, axis=1, keepdims=True)
    )
    high = decoder_grads.astype(BF)
    low = (decoder_grads - high.astype(F32)).astype(BF)
    grads[z, x] = (nn(member_bf, high) + nn(member_bf, low)).astype(BF)

    grads_g = gather(grads, cut_cols, True)
    next(grads_g)
    state_grads[...] = decoder_grads

    def sent(copies):
        for copy in copies:
            copy.wait_send()

    @pl.when(z == y)
    def _():
        sent(spread_in + spread_out)

    early = len(sends) - 20
    sent(sends[:early])
    run(grads_g)

    def backward(i):
        rows = grads[i].reshape(ROWS, E)
        hidden_grads = nt(rows[:, :EH], fold_d[0].reshape(FB, EH)) + nt(rows[:, EH:], fold_d[1].reshape(FB, EH))
        g_gate[i] = (hidden_grads * gate_c[i]).astype(BF)
        g_up[i] = (hidden_grads * up_c[i]).astype(BF)
        g_mix[i] = nt(rows, w_out[...]).astype(BF)

    def fill_grads(i, h):
        term = (
            nt(g_gate[i], fold_g[h].reshape(EH, FB))
            + nt(g_up[i], fold_u[h].reshape(EH, FB))
            + nt(g_mix[i], w_in[h * EH:(h + 1) * EH, :])
        )
        qout[i, :, :, h * EH:(h + 1) * EH] = term.astype(BF).reshape(SIDE, SLOTS, EH)

    pooled_grads = scatter_sum(1, backward, fill_grads, qout)
    spread_grads[...] = nn(member_t_bf, pooled_grads) / byte_divisor

    sent(sends[early:])
    assert count[0] <= N_SEMS


def body(
    states, patch_of, targets, cotangent, w_in, w_gate, w_up, w_down, w_out, head_gain, w_head
):
    n, E = states.shape
    DT = w_in.shape[1]
    DG, FB = w_gate.shape
    V = w_head.shape[1]
    EH = E // 2
    ER, FR, OR = EH // SIDE, FB // SIDE, DT // SIDE
    ROWS = SIDE * SLOTS
    vmem = lambda *shape: pltpu.VMEM(shape, BF)
    vmem32 = lambda *shape: pltpu.VMEM(shape, F32)
    scratch = [
        vmem(2, FB, DG), vmem(2, FB, DG), vmem(2, FB, DG), vmem(E, V),
        vmem(SIDE, SIDE, ER, DT), vmem(SIDE, SIDE, OR, EH),
        vmem(SIDE, SIDE, SLOTS, E),
        vmem(2, SIDE, ER, FB), vmem(2, SIDE, ER, FB), vmem(2, SIDE, FR, EH),
        vmem(SIDE, ER, FB), vmem(SIDE, ER, FB), vmem(SIDE, FR, EH),
        vmem(2, ER, FB), vmem(2, ER, FB), vmem(2, FR, EH),
        vmem(2, ER, FB), vmem(2, ER, FB), vmem(2, FR, EH),
        vmem(SIDE, ROWS, DT),
        vmem32(SIDE, ROWS, FB), vmem32(SIDE, ROWS, FB),
        vmem(SIDE, ROWS, FB),
        vmem(SIDE, SIDE, SLOTS, E), vmem(SIDE, SIDE, SLOTS, E),
        vmem(SIDE, ROWS, FB), vmem(SIDE, ROWS, FB), vmem(SIDE, ROWS, DT),
        vmem(SIDE, SIDE, SLOTS, E),
        vmem(2, 2, SIDE - 1, SIDE, SLOTS, EH), vmem(2, 2, SIDE - 1, SLOTS, EH),
        vmem(2, 2, SIDE, SLOTS, EH),
        pltpu.SemaphoreType.DMA((N_SEMS,)), pltpu.SemaphoreType.DMA((N_SEMS,)),
        pltpu.SemaphoreType.DMA((4,)),
    ]
    near = pl.BlockSpec(memory_space=pltpu.VMEM)
    away = pl.BlockSpec(memory_space=pl.ANY)
    log_probs, decoder_grads, spread_grads = pl.pallas_call(
        kernel,
        out_shape=(jax.ShapeDtypeStruct((1, n), F32),) + (jax.ShapeDtypeStruct((n, E), F32),) * 2,
        in_specs=[near] * 5 + [away] * 3 + [near] * 2 + [away],
        out_specs=(near, near, near),
        scratch_shapes=scratch,
        compiler_params=pltpu.CompilerParams(
            collective_id=0, has_side_effects=True, vmem_limit_bytes=60 * 2**20
        ),
        name="patch_step",
    )(
        states, patch_of.reshape(1, n), targets.reshape(1, n), cotangent.reshape(1, n),
        w_in, w_gate.T, w_up.T, w_down, w_out, head_gain, w_head,
    )
    return log_probs.reshape(n), decoder_grads + spread_grads


def solution(mesh):
    return jax.shard_map(
        body,
        mesh=mesh,
        in_specs=(
            P(("grp", "tp"), None),
            P(("grp", "tp")),
            P(("grp", "tp")),
            P(("grp", "tp")),
            P(None, "tp"),
            P("grp", "tp"),
            P("grp", "tp"),
            P("tp", "grp"),
            P("tp", None),
            P(),
            P(),
        ),
        out_specs=(P(("grp", "tp")), P(("grp", "tp"), None)),
        check_vma=False,
    )
```

```python
import jax
import jax.numpy as jnp
from jax import lax
from jax.experimental import pallas as pl
from jax.experimental.pallas import tpu as pltpu
from jax.sharding import PartitionSpec as P

BF = jnp.bfloat16
F32 = jnp.float32
MESH = pl.DeviceIdType.MESH
SIDE = 4
SLOTS = 48
N_SEMS = 256


def nn(a, b):
    return lax.dot_general(a, b, (((1,), (0,)), ((), ())), preferred_element_type=F32)


def nt(a, b):
    return lax.dot_general(a, b, (((1,), (1,)), ((), ())), preferred_element_type=F32)


def wrap(v):
    return lax.rem(v, SIDE)


def kernel(
    states, patch_of, targets, cotangent, w_in, w_gate, w_up, w_down, w_out, gain, w_head,
    log_probs, state_grads, spread_grads,
    raw_g, raw_u, raw_d, head_w, slab_in, slab_out, pool, fold_g, fold_u, fold_d,
    part_g, part_u, part_d, edge_g, edge_u, edge_d, mid_g, mid_u, mid_d,
    act, gate_c, up_c, hid, pout, qout, g_gate, g_up, g_mix, grads,
    rs1, rs2, mid1,
    ssem, rsem, lsem,
):
    N, E = states.shape
    EH = E // 2
    FB = w_gate.shape[0]
    DT = w_in.shape[1]
    ER = EH // SIDE
    FR = FB // SIDE
    OR = DT // SIDE
    ROWS = SIDE * SLOTS

    g = lax.axis_index("grp")
    t = lax.axis_index("tp")
    y, c = g // 2, g % 2
    z, x = t // SIDE, t % SIDE

    def X(d):
        return (g, SIDE * z + wrap(x + d))

    def Z(d):
        return (g, SIDE * wrap(z + d) + x)

    def Y(d):
        return (2 * wrap(y + d) + c, t)

    partner = (2 * y + (1 - c), t)

    sends = []
    count = [0]

    def new_sem():
        count[0] += 1
        return count[0] - 1

    def remote(src, dst, device):
        i = new_sem()
        copy = pltpu.make_async_remote_copy(
            src_ref=src, dst_ref=dst, send_sem=ssem.at[i], recv_sem=rsem.at[i],
            device_id=device, device_id_type=MESH,
        )
        copy.start()
        sends.append(copy)
        return copy

    def arrive(copies):
        for copy in copies:
            copy.wait_recv()

    barrier = pltpu.get_barrier_semaphore()
    peers = [X(d) for d in (1, 2, 3)] + [Z(d) for d in (1, 2, 3)] + [Y(1), Y(3), partner]
    for peer in peers:
        pl.semaphore_signal(barrier, 1, device_id=peer, device_id_type=MESH)

    local = [
        pltpu.make_async_copy(src, dst, lsem.at[i])
        for i, (src, dst) in enumerate(
            ((w_gate, raw_g.at[c]), (w_up, raw_u.at[c]), (w_down, raw_d.at[c]), (w_head, head_w))
        )
    ]
    for copy in local:
        copy.start()

    def column(row):
        return jnp.transpose(jnp.broadcast_to(row, (N, N)))[:, :1]

    member = patch_of[...] == lax.broadcasted_iota(jnp.int32, (SLOTS, N), 0)
    member_bf = member.astype(BF)
    divisor = jnp.maximum(jnp.sum(member.astype(F32), axis=1, keepdims=True), 1.0)
    pool[z, x] = (nn(member_bf, states[...]) / divisor).astype(BF)

    pl.semaphore_wait(barrier, len(peers))

    def spread(src_of, dst_of):
        first = [new_sem() for _ in range(SIDE)]
        out = []
        for d in range(1, SIDE):
            zz = wrap(z + d)
            out.append(
                pltpu.make_async_remote_copy(
                    src_ref=src_of(zz), dst_ref=dst_of(zz), send_sem=ssem.at[first[d]],
                    recv_sem=rsem.at[first[0]], device_id=Z(d), device_id_type=MESH,
                )
            )
        return out

    spread_in = spread(
        lambda zz: w_in.at[pl.ds(pl.multiple_of(c * EH + zz * ER, 16), ER), :],
        lambda zz: slab_in.at[zz, x],
    )

    spread_out = spread(
        lambda zz: w_out.at[
            pl.ds(pl.multiple_of(zz * OR, 16), OR), pl.ds(pl.multiple_of(c * EH, 128), EH)
        ],
        lambda zz: slab_out.at[zz, x],
    )

    def spread_start(copies):
        @pl.when(z == y)
        def _():
            for copy in copies:
                copy.start()

    def spread_arrive(copies):
        @pl.when(z != y)
        def _():
            copies[0].wait_recv()

    spread_start(spread_in)
    spread_start(spread_out)

    swap = []
    for src, dst in ((w_gate, raw_g), (w_up, raw_u), (w_down, raw_d)):
        swap.append(remote(src, dst.at[c], partner))

    @pl.when(z == y)
    def _():
        slab_in[z, x] = w_in[pl.ds(pl.multiple_of(c * EH + z * ER, 16), ER), :]
        piece = w_out[pl.ds(pl.multiple_of(z * OR, 16), OR), :]
        slab_out[z, x] = jnp.where(c == 0, piece[:, :EH], piece[:, EH:])

    def gather(buf, cut, ring):
        def slot(h, f, s, piece=None):
            at = (wrap(z + s + 4), wrap(x + f + 4)) if h == 0 else (wrap(z + f + 4), wrap(x + s + 4))
            return buf.at[at + cut(h, piece)]

        def first(h, d):
            return X(d) if h == 0 else Z(d)

        def second(h, d):
            return Z(d) if h == 0 else X(d)

        def send(ref, device):
            return remote(ref, ref, device)

        ways = (1, 3) if ring else (1, 3, 2)
        one, two, last = {}, {}, []
        for d in (2, 1, 3):
            for h in range(2):
                one[h, d] = send(slot(h, 0, 0), first(h, d))
        for e in ways:
            for h in range(2):
                two[h, 0, e] = send(slot(h, 0, 0), second(h, e))
        yield
        for d in (1, 3, 2):
            for h in range(2):
                one[h, d].wait_recv()
                for e in ways:
                    two[h, d, e] = send(slot(h, -d, 0), second(h, e))
        yield
        if ring:
            for d in (0, 1, 3, 2):
                for e in ways:
                    for h in range(2):
                        two[h, d, e].wait_recv()
                        last.append(send(slot(h, -d, -e, e // 2), second(h, e)))
                yield
            arrive(last)
        else:
            arrive(two.values())

    def cut_rows(rows, split):
        def cut(h, piece):
            lo, hi = h * rows // 2, (h + 1) * rows // 2
            mid = lo + split[h]
            if piece == 0:
                hi = mid
            elif piece == 1:
                lo = mid
            return (slice(lo, hi), slice(None))
        return cut

    def cut_cols(h, piece):
        lo, hi = h * EH, (h + 1) * EH
        mid = lo + (384 if h == 0 else 256)
        if piece == 0:
            hi = mid
        elif piece == 1:
            lo = mid
        return (slice(None), slice(lo, hi))

    def run(gen):
        for _ in gen:
            pass

    in_g = gather(slab_in, cut_rows(ER, (48, 32)), False)
    out_g = gather(slab_out, cut_rows(OR, (16, 16)), False)
    pool_g = gather(pool, cut_cols, False)

    spread_arrive(spread_in)
    next(in_g)
    next(in_g)
    spread_arrive(spread_out)
    next(out_g)
    run(in_g)
    arrive(swap[:2])
    for copy in local[:2]:
        copy.wait()

    def block_in(raw):
        def f():
            total = jnp.zeros((EH, FB), F32)
            for xx in range(SIDE):
                lo = (xx % 2) * DT
                total += nt(slab_in[:, xx].reshape(EH, DT), raw[xx // 2, :, lo:lo + DT])
            return total.astype(BF).reshape(SIDE, ER, FB)
        return f

    def block_down():
        total = jnp.zeros((FB, EH), F32)
        for xx in range(SIDE):
            lo = (xx % 2) * DT
            total += nn(raw_d[xx // 2, :, lo:lo + DT], slab_out[:, xx].reshape(DT, EH))
        return total.astype(BF).reshape(SIDE, FR, EH)

    class Fold:
        def __init__(self, block, part, edge, mid, out, split):
            self.block, self.part, self.edge, self.mid, self.split = block, part, edge, mid, split
            self.out = out

        def step_1(self):
            if self.block is not None:
                self.part[...] = self.block()
            s = self.split
            far = wrap(y + 2)
            self.one = [
                remote(self.part.at[far, :s], self.edge.at[0, :s], Y(1)),
                remote(self.part.at[far, s:], self.edge.at[1, s:], Y(3)),
            ]

        def step_2(self):
            s = self.split
            right, left = wrap(y + 1), wrap(y + 3)
            self.one[0].wait_recv()
            self.part[right, :s] = (self.part[right, :s].astype(F32) + self.edge[0, :s].astype(F32)).astype(BF)
            two = [remote(self.part.at[right], self.mid.at[0], Y(1))]
            self.one[1].wait_recv()
            self.part[left, s:] = (self.part[left, s:].astype(F32) + self.edge[1, s:].astype(F32)).astype(BF)
            self.two = two + [remote(self.part.at[left], self.mid.at[1], Y(3))]

        def step_3(self):
            arrive(self.two)
            total = self.part[y].astype(F32) + self.mid[0].astype(F32) + self.mid[1].astype(F32)
            own = self.out(y)
            own[...] = total.astype(BF)
            self.three = [remote(own, own, Y(1)), remote(own, own, Y(3))]
            self.cross = [remote(own, own, partner)]

        def step_4(self):
            s = self.split
            self.three[0].wait_recv()
            low = self.out(wrap(y + 3))
            four = [remote(low.at[:s], low.at[:s], Y(1))]
            self.cross.append(remote(low, low, partner))
            self.three[1].wait_recv()
            high = self.out(wrap(y + 1))
            four.append(remote(high.at[s:], high.at[s:], Y(3)))
            self.cross.append(remote(high, high, partner))
            self.four = four

        def step_5(self):
            arrive(self.four)
            far = self.out(wrap(y + 2))
            self.cross.append(remote(far, far, partner))
            arrive(self.cross)

    gate_f = Fold(block_in(raw_g), part_g, edge_g, mid_g, lambda yy: fold_g.at[c, yy], ER // 2)
    up_f = Fold(block_in(raw_u), part_u, edge_u, mid_u, lambda yy: fold_u.at[c, yy], ER // 2)

    def fold_down(rows, split):
        return Fold(
            None, part_d.at[:, rows], edge_d.at[:, rows], mid_d.at[:, rows],
            lambda yy: fold_d.at[c, yy, rows], split,
        )

    downs = [fold_down(slice(0, 64), 32), fold_down(slice(64, FR), 32)]

    def down_step(name):
        for fold in downs:
            getattr(fold, name)()

    gate_f.step_1()
    up_f.step_1()
    next(out_g)
    next(pool_g)
    gate_f.step_2()
    up_f.step_2()

    patch_col = column(patch_of[...])
    member_t = patch_col == lax.broadcasted_iota(jnp.int32, (N, SLOTS), 1)
    member_t_bf = member_t.astype(BF)
    divisor_row = jnp.maximum(jnp.sum(member_t.astype(F32), axis=0, keepdims=True), 1.0)
    byte_divisor = jnp.sum(jnp.where(member_t, divisor_row, 0.0), axis=1, keepdims=True)
    target_col = column(targets[...])
    weight_col = column(cotangent[...])

    run(out_g)
    arrive(swap[2:])
    local[2].wait()
    part_d[...] = block_down()
    down_step("step_1")
    next(pool_g)
    gate_f.step_3()
    up_f.step_3()
    down_step("step_2")
    gate_f.step_4()
    up_f.step_4()
    down_step("step_3")
    gate_f.step_5()
    up_f.step_5()
    run(pool_g)

    def forward(i, carry):
        rows = pool[i].reshape(ROWS, E)
        act[i] = nn(rows, w_in[...]).astype(BF)
        gate_pre = nn(rows, fold_g[...].reshape(E, FB))
        up_pre = nn(rows, fold_u[...].reshape(E, FB))
        s = 1.0 / (1.0 + jnp.exp(-gate_pre))
        silu = gate_pre * s
        hid[i] = (silu * up_pre).astype(BF)
        gate_c[i] = up_pre * s * (1.0 + gate_pre * (1.0 - s))
        up_c[i] = silu
        return carry

    down_step("step_4")
    lax.fori_loop(0, SIDE, forward, 0)
    down_step("step_5")

    def scatter_sum(k, prepare, fill, buf):
        one, two = {}, {}

        def cols(h):
            return slice(h * EH, (h + 1) * EH)

        def send_one(h, p, q):
            at = (wrap(z + p), wrap(x + q)) if h == 0 else (wrap(z + q), wrap(x + p))
            one[h, q, p] = remote(
                buf.at[at + (slice(None), cols(h))], rs1.at[k, h, p - 1, q], Z(p) if h == 0 else X(p)
            )

        def send_all(h, q):
            for p in (2, 1, 3):
                send_one(h, p, q)

        prepare(wrap(z + 2))
        fill(wrap(z + 2), 0)
        send_one(0, 2, 2)
        fill(wrap(z + 2), 1)
        send_all(1, 2)
        for d in (1, 3):
            prepare(wrap(z + d))
            fill(wrap(z + d), 0)
            send_one(0, d, 2)
        send_all(0, 1)
        fill(wrap(z + 1), 1)
        send_all(1, 1)
        send_all(0, 3)
        fill(wrap(z + 3), 1)
        send_all(1, 3)
        send_all(0, 0)
        prepare(z)
        fill(z, 1)
        send_all(1, 0)
        fill(z, 0)
        halves = {}
        for q in (2, 1, 3, 0):
            for h in (1, 0):
                at = (z, wrap(x + q)) if h == 0 else (wrap(z + q), x)
                for p in (1, 3, 2):
                    one[h, q, p].wait_recv()
                total = buf[at + (slice(None), cols(h))].astype(F32)
                for p in range(SIDE - 1):
                    total += rs1[k, h, p, q].astype(F32)
                if q:
                    mid1[k, h, q] = total.astype(BF)
                    two[h, q] = remote(
                        mid1.at[k, h, q], rs2.at[k, h, q - 1], X(q) if h == 0 else Z(q)
                    )
                else:
                    halves[h] = total
        for h in range(2):
            total = halves[h]
            for q in (1, 3, 2):
                two[h, q].wait_recv()
                total += rs2[k, h, q - 1].astype(F32)
            halves[h] = total.astype(BF)
        return jnp.concatenate([halves[0], halves[1]], axis=1)

    def fill_out(i, h):
        term = nn(hid[i], fold_d[h].reshape(FB, EH)) + nn(act[i], w_out[:, h * EH:(h + 1) * EH])
        pout[i, :, :, h * EH:(h + 1) * EH] = term.astype(BF).reshape(SIDE, SLOTS, EH)

    patch_out = scatter_sum(0, lambda i: None, fill_out, pout)

    decoder_in = states[...].astype(F32) + nn(member_t_bf, patch_out)
    inverse = lax.rsqrt(jnp.mean(decoder_in * decoder_in, axis=1, keepdims=True) + 1e-06)
    normal_part = decoder_in * inverse
    gains = gain[...].reshape(1, E)
    normed = (normal_part * gains).astype(BF)
    local[3].wait()
    logits = nn(normed, head_w[...])
    log_total = jnp.log(jnp.sum(jnp.exp(logits), axis=1, keepdims=True))
    is_target = target_col == lax.broadcasted_iota(jnp.int32, logits.shape, 1)
    chosen = jnp.sum(jnp.where(is_target, logits, 0.0), axis=1, keepdims=True)
    log_probs[...] = jnp.transpose(jnp.broadcast_to(chosen - log_total, (N, N)))[:1, :]
    probs = jnp.exp(logits - log_total)
    logit_grads = (weight_col * (is_target.astype(F32) - probs)).astype(BF)
    scaled = nt(logit_grads, head_w[...]) * gains
    decoder_grads = inverse * (
        scaled - normal_part * jnp.mean(scaled * normal_part, axis=1, keepdims=True)
    )
    high = decoder_grads.astype(BF)
    low = (decoder_grads - high.astype(F32)).astype(BF)
    grads[z, x] = (nn(member_bf, high) + nn(member_bf, low)).astype(BF)

    grads_g = gather(grads, cut_cols, True)
    next(grads_g)
    state_grads[...] = decoder_grads

    def sent(copies):
        for copy in copies:
            copy.wait_send()

    @pl.when(z == y)
    def _():
        sent(spread_in + spread_out)

    early = len(sends) - 20
    sent(sends[:early])
    run(grads_g)

    def backward(i):
        rows = grads[i].reshape(ROWS, E)
        hidden_grads = nt(rows[:, :EH], fold_d[0].reshape(FB, EH)) + nt(rows[:, EH:], fold_d[1].reshape(FB, EH))
        g_gate[i] = (hidden_grads * gate_c[i]).astype(BF)
        g_up[i] = (hidden_grads * up_c[i]).astype(BF)
        g_mix[i] = nt(rows, w_out[...]).astype(BF)

    def fill_grads(i, h):
        term = (
            nt(g_gate[i], fold_g[h].reshape(EH, FB))
            + nt(g_up[i], fold_u[h].reshape(EH, FB))
            + nt(g_mix[i], w_in[h * EH:(h + 1) * EH, :])
        )
        qout[i, :, :, h * EH:(h + 1) * EH] = term.astype(BF).reshape(SIDE, SLOTS, EH)

    pooled_grads = scatter_sum(1, backward, fill_grads, qout)
    spread_grads[...] = nn(member_t_bf, pooled_grads) / byte_divisor

    sent(sends[early:])
    assert count[0] <= N_SEMS


def body(
    states, patch_of, targets, cotangent, w_in, w_gate, w_up, w_down, w_out, head_gain, w_head
):
    n, E = states.shape
    DT = w_in.shape[1]
    DG, FB = w_gate.shape
    V = w_head.shape[1]
    EH = E // 2
    ER, FR, OR = EH // SIDE, FB // SIDE, DT // SIDE
    ROWS = SIDE * SLOTS
    vmem = lambda *shape: pltpu.VMEM(shape, BF)
    vmem32 = lambda *shape: pltpu.VMEM(shape, F32)
    scratch = [
        vmem(2, FB, DG), vmem(2, FB, DG), vmem(2, FB, DG), vmem(E, V),
        vmem(SIDE, SIDE, ER, DT), vmem(SIDE, SIDE, OR, EH),
        vmem(SIDE, SIDE, SLOTS, E),
        vmem(2, SIDE, ER, FB), vmem(2, SIDE, ER, FB), vmem(2, SIDE, FR, EH),
        vmem(SIDE, ER, FB), vmem(SIDE, ER, FB), vmem(SIDE, FR, EH),
        vmem(2, ER, FB), vmem(2, ER, FB), vmem(2, FR, EH),
        vmem(2, ER, FB), vmem(2, ER, FB), vmem(2, FR, EH),
        vmem(SIDE, ROWS, DT),
        vmem32(SIDE, ROWS, FB), vmem32(SIDE, ROWS, FB),
        vmem(SIDE, ROWS, FB),
        vmem(SIDE, SIDE, SLOTS, E), vmem(SIDE, SIDE, SLOTS, E),
        vmem(SIDE, ROWS, FB), vmem(SIDE, ROWS, FB), vmem(SIDE, ROWS, DT),
        vmem(SIDE, SIDE, SLOTS, E),
        vmem(2, 2, SIDE - 1, SIDE, SLOTS, EH), vmem(2, 2, SIDE - 1, SLOTS, EH),
        vmem(2, 2, SIDE, SLOTS, EH),
        pltpu.SemaphoreType.DMA((N_SEMS,)), pltpu.SemaphoreType.DMA((N_SEMS,)),
        pltpu.SemaphoreType.DMA((4,)),
    ]
    near = pl.BlockSpec(memory_space=pltpu.VMEM)
    away = pl.BlockSpec(memory_space=pl.ANY)
    log_probs, decoder_grads, spread_grads = pl.pallas_call(
        kernel,
        out_shape=(jax.ShapeDtypeStruct((1, n), F32),) + (jax.ShapeDtypeStruct((n, E), F32),) * 2,
        in_specs=[near] * 5 + [away] * 3 + [near] * 2 + [away],
        out_specs=(near, near, near),
        scratch_shapes=scratch,
        compiler_params=pltpu.CompilerParams(
            collective_id=0, has_side_effects=True, vmem_limit_bytes=60 * 2**20
        ),
        name="patch_step",
    )(
        states, patch_of.reshape(1, n), targets.reshape(1, n), cotangent.reshape(1, n),
        w_in, w_gate.T, w_up.T, w_down, w_out, head_gain, w_head,
    )
    return log_probs.reshape(n), decoder_grads + spread_grads


def solution(mesh):
    return jax.shard_map(
        body,
        mesh=mesh,
        in_specs=(
            P(("grp", "tp"), None),
            P(("grp", "tp")),
            P(("grp", "tp")),
            P(("grp", "tp")),
            P(None, "tp"),
            P("grp", "tp"),
            P("grp", "tp"),
            P("tp", "grp"),
            P("tp", None),
            P(),
            P(),
        ),
        out_specs=(P(("grp", "tp")), P(("grp", "tp"), None)),
        check_vma=False,
    )
```
